768 devices in a mesh: space: 48 (over x, z_lo, core), dp: 16 (over z_hi, y).
Axes of the slice: x: 4, y: 8, z: 12 (z_hi: 2, z_lo: 6; z = z_hi * 6 + z_lo), core: 2. Of those that a mesh axis runs over, the one named last changes fastest.
Arguments:
- features: bfloat16 [32, 48, 72, 2048], P('dp', 'space'), may hold values from -6 to 6
- pointwise: bfloat16 [2, 2048, 256], P(None, 'dp'), may hold values from -0.125 to 0.125
- depthwise: bfloat16 [2, 9, 2048], P(None, None, 'dp'), may hold values from -2 to 2
- cotangent: bfloat16 [32, 48, 72, 512], P('dp', 'space'), may hold values from -6 to 6
Outputs:
- branches_out: bfloat16 [32, 48, 72, 512], P('dp', 'space')
- feature_grad: bfloat16 [32, 48, 72, 2048], P('dp', 'space')
- pointwise_grad: float32 [2, 2048, 256], P(None, 'dp')
- depthwise_grad: float32 [2, 9, 2048], P(None, None, 'dp')
The draws below stay inside these ranges and needn't reach their ends.
All inputs are finite; a program needn't handle non-finite values.
Results may differ from the reference program's by a relative error of at most 0.014.
Values may be sent and summed in bfloat16 or wider, within the bound.
A program may use at most 32 MiB of HBM per device.

```python
import jax
import jax.numpy as jnp
from jax import lax

C = 2048
CO = 256
H = 48
W = 72
RATE_A = 12
RATE_B = 24
IMG_DEV = 2
IMAGES = 32
N_SPACE = 48
N_DP = 16


def raised(array, own_key, source, target, blocks, factor):
    owner, partner = [(jnp.arange(array.shape[axis_at]) // (array.shape[axis_at] // blocks)).reshape([-1 if axis == axis_at else 1 for axis in range(array.ndim)]) for axis_at in (source, target)]
    chosen = jax.random.permutation(own_key, blocks)[partner]
    strong = (owner == chosen) | (owner == (partner + blocks // 2) % blocks)
    return jnp.where(strong, factor * array, array)


def steps_of(rng, dims, pieces, smallest, top_value):
    level, own = 1.0, jax.random.fold_in(rng, 6)
    for dim, parts in pieces:
        draws = jnp.exp(jax.random.uniform(jax.random.fold_in(own, dim), (parts,), jnp.float32, smallest / len(pieces), top_value / len(pieces)))
        level = level * jnp.repeat(draws, dims[dim] // parts).reshape([-1 if axis == dim else 1 for axis in range(len(dims))])
    return level


def bell_draw(rng, extent, deviation, reach, pieces=(), held_as=jnp.bfloat16):
    gain = steps_of(rng, extent, pieces, -0.22, 0.18) if pieces else 1.0
    drawn = jax.random.normal(rng, extent, jnp.float32) * deviation * gain
    return jnp.minimum(jnp.maximum(drawn, -reach), reach).astype(held_as)


def bell_draw_with(stream_key, shape, deviation, bound, pieces, heavy, held_as=jnp.bfloat16):
    array = deviation * jax.random.normal(stream_key, shape, jnp.float32)
    if pieces:
        array = array * steps_of(stream_key, shape, pieces, -0.22, 0.18)
    return jnp.clip(raised(array, jax.random.fold_in(stream_key, 3), *heavy), -bound, bound).astype(held_as)


def setup_inputs(seed: int = 0) -> dict:
    key_of = jax.random.split(jax.random.key(seed), 5)
    features = bell_draw_with(key_of[0], (IMAGES, H, W, C), 1.0, 6.0, ((0, 16), (1, 48)), (0, 3, 16, 2.0))
    pointwise = bell_draw(key_of[1], (2, C, CO), C ** -0.5, 0.125, ((1, 16),))
    depthwise = bell_draw(key_of[2], (2, 9, C), 0.33, 2.0, ((2, 16),))
    cotangent = bell_draw(key_of[3], (IMAGES, H, W, 2 * CO), 1.0, 6.0, ((0, 16), (1, 48)))
    return dict(features=features, pointwise=pointwise, depthwise=depthwise, cotangent=cotangent)


def shifted(field, rate, up, side):
    padded = jnp.pad(field, ((0, 0), (rate, rate), (rate, rate), (0, 0)))
    row_start = rate + up * rate
    col_start = rate + side * rate
    return padded[:, row_start:row_start + H, col_start:col_start + W, :]

def group_pass(feat_group, cot_group, pointwise, depthwise):
    rows_dev = H // N_SPACE
    outputs = []
    grad_total = jnp.zeros(feat_group.shape, jnp.float32)
    w_parts = []
    k_parts = []
    for branch, rate in enumerate((RATE_A, RATE_B)):
        dsum = jnp.zeros(feat_group.shape, jnp.float32)
        for up in (-1, 0, 1):
            for side in (-1, 0, 1):
                tap = (up + 1) * 3 + (side + 1)
                dsum = dsum + shifted(feat_group, rate, up, side).astype(jnp.float32) * depthwise[branch, tap].astype(jnp.float32)
        dconv = dsum.astype(jnp.bfloat16)
        flat = dconv.reshape(-1, C)
        pre = jnp.dot(flat, pointwise[branch], preferred_element_type=jnp.float32)
        sig = jax.nn.sigmoid(pre)
        outputs.append((pre * sig).reshape(IMG_DEV, H, W, CO).astype(jnp.bfloat16))
        cot_part = cot_group[..., branch * CO:(branch + 1) * CO].reshape(-1, CO).astype(jnp.float32)
        gpre = (cot_part * sig * (1.0 + pre * (1.0 - sig))).astype(jnp.bfloat16)
        gdconv = lax.dot_general(gpre, pointwise[branch], (((1,), (1,)), ((), ())), preferred_element_type=jnp.float32).astype(jnp.bfloat16)
        gdconv = gdconv.reshape(feat_group.shape)
        blocks_d = dconv.reshape(IMG_DEV, N_SPACE, rows_dev, W, C).astype(jnp.float32)
        blocks_g = gpre.reshape(IMG_DEV, N_SPACE, rows_dev, W, CO).astype(jnp.float32)
        wblock = jnp.einsum('asrwc,asrwo->sco', blocks_d, blocks_g)
        w_parts.append(lax.optimization_barrier(jnp.sum(wblock.astype(jnp.bfloat16).astype(jnp.float32), axis=0)))
        gd_blocks = gdconv.reshape(IMG_DEV, N_SPACE, rows_dev, W, C).astype(jnp.float32)
        tap_rows = []
        for up in (-1, 0, 1):
            for side in (-1, 0, 1):
                tap = (up + 1) * 3 + (side + 1)
                src = shifted(feat_group, rate, up, side).reshape(IMG_DEV, N_SPACE, rows_dev, W, C).astype(jnp.float32)
                kblock = lax.optimization_barrier(jnp.sum(src * gd_blocks, axis=(0, 2, 3)))
                tap_rows.append(lax.optimization_barrier(jnp.sum(kblock.astype(jnp.bfloat16).astype(jnp.float32), axis=0)))
                grad_total = grad_total + shifted(gdconv, rate, -up, -side).astype(jnp.float32) * depthwise[branch, tap].astype(jnp.float32)
        k_parts.append(jnp.stack(tap_rows))
    joined = jnp.concatenate(outputs, axis=-1)
    return (joined, grad_total.astype(jnp.bfloat16), jnp.stack(w_parts), jnp.stack(k_parts))

def reference(features, pointwise, depthwise, cotangent):
    feat_groups = features.reshape(N_DP, IMG_DEV, H, W, C)
    cot_groups = cotangent.reshape(N_DP, IMG_DEV, H, W, 2 * CO)

    def one_group(pair):
        return group_pass(pair[0], pair[1], pointwise, depthwise)
    joined, grads, w_sums, k_sums = lax.map(one_group, (feat_groups, cot_groups))
    factor = 1.0 / jnp.sqrt(jnp.float32(IMG_DEV * N_DP * H * W))
    branches_out = joined.reshape(IMG_DEV * N_DP, H, W, 2 * CO)
    feature_grad = grads.reshape(IMG_DEV * N_DP, H, W, C)
    pointwise_grad = lax.optimization_barrier(jnp.sum(w_sums, axis=0)) * factor
    depthwise_grad = lax.optimization_barrier(jnp.sum(k_sums, axis=0)) * factor
    return (branches_out, feature_grad, pointwise_grad, depthwise_grad)
```

```python
import jax
import jax.numpy as jnp
from jax import lax
from jax.experimental import pallas as pl
from jax.experimental.pallas import tpu as pltpu
from jax.sharding import PartitionSpec as P

C = 2048
CO = 256
CELLS = 144
LANES = 128
PART = 512
BF16 = jnp.bfloat16
F32 = jnp.float32
MESH = pl.DeviceIdType.MESH
FACTOR = 1.0 / (110592.0**0.5)


def device_at(x, z_low, core, z_high, y):
    return {"space": (x * 6 + z_low) * 2 + core, "dp": z_high * 8 + y}


def local_wait(ref, sem):
    pltpu.make_async_copy(ref, ref, sem).wait()


def kernel(
    feat, pw, kin, cot,
    out, fgrad, pgrad, kgrad,
    rows, wide, moved, taps, dcv, wts, away_w, away_k,
    own_pre, send_pre, got_pre, gpre, ga, ga_moved, gb, fg_send,
    wg_wide, wg, wg_core, wg_y, wg_y_got, wg_z, wg_z_got, wg_red,
    kg, kg_core, kg_y, kg_y_got, kg_z, kg_z_got, kg_red, fin, kfin,
    f_send, f_recv, own_sem, a_send, a_recv, w_send, w_recv, k_send, k_recv, wc_send, wc_recv,
    p_send, p_recv, g_send, g_recv, o_send, o_recv,
    c_send, c_recv, y_send, y_recv, z_send, z_recv, b_send, b_recv, e_send, e_recv,
    kc_send, kc_recv, ky_send, ky_recv, kz_send, kz_recv, kb_send, kb_recv, ke_send, ke_recv,
):
    space = lax.axis_index("space")
    dp = lax.axis_index("dp")
    x = space // 12
    zl = (space // 2) % 6
    core = space % 2
    zh = dp // 8
    y = dp % 8
    z = zh * 6 + zl
    plane = y // 2
    at_home = x == plane
    mate = device_at(x, zl, 1 - core, zh, y)
    sent = []

    def remote(src, dst, send_sem, recv_sem, target):
        return pltpu.make_async_remote_copy(
            src_ref=src, dst_ref=dst, send_sem=send_sem, recv_sem=recv_sem,
            device_id=target, device_id_type=MESH,
        )

    def send(src, dst, send_sem, recv_sem, target):
        copy = remote(src, dst, send_sem, recv_sem, target)
        copy.start()
        sent.append((None, copy))

    def send_if(cond, src, dst, send_sem, recv_sem, target):
        copy = remote(src, dst, send_sem, recv_sem, target)
        here = pltpu.make_async_copy(src, dst, recv_sem)

        @pl.when(cond)
        def _():
            copy.start()

        @pl.when(jnp.logical_not(cond))
        def _():
            here.start()

        sent.append((cond, copy))

    def x_peer(k):
        return device_at((x + k) % 4, zl, core, zh, y)

    def z_peer(k):
        other = (z + k) % 12
        return device_at(x, other % 6, core, other // 6, y)

    sides = (slice(0, 256), slice(256, 512))

    def channels(of_x, side):
        return pl.ds(pl.multiple_of(side * 1024 + of_x * 256, 256), 256)

    barrier = pltpu.get_barrier_semaphore()

    def greet(target):
        pl.semaphore_signal(barrier, inc=1, device_id=target, device_id_type=MESH)

    count = 0
    for k in (1, 3, 2):
        greet(x_peer(k))
        count += 1
    greet(mate)
    count += 1
    for k in range(1, 12):
        greet(z_peer(k))
        count += 1
    for k in range(1, 8):
        greet(device_at(plane, zl, core, zh, (y + k) % 8))
        count += 1
    for other in range(4):
        for near in range(2):
            target_y = 2 * x + near
            same = jnp.logical_and(other == x, target_y == y)

            @pl.when(jnp.logical_not(same))
            def _(other=other, target_y=target_y):
                greet(device_at(other, zl, core, zh, target_y))

    @pl.when(jnp.logical_not(at_home))
    def _():
        greet(device_at(plane, zl, core, zh, y))

    count += 9
    moved[...] = jnp.zeros_like(moved)
    ga_moved[...] = jnp.zeros_like(ga_moved)
    kg[...] = jnp.zeros_like(kg)
    pl.semaphore_wait(barrier, count - 2 * at_home.astype(jnp.int32))

    for k in (2, 1, 3):
        for side in range(2):
            send(
                feat.at[:, channels((x + k) % 4, side)], rows.at[x, :, sides[side]],
                f_send.at[side, k], f_recv.at[side, k], x_peer(k),
            )
    own_rows = [
        pltpu.make_async_copy(
            feat.at[:, channels(x, side)], rows.at[x, :, sides[side]], own_sem.at[side]
        )
        for side in range(2)
    ]
    for copy in own_rows:
        copy.start()

    piece = pl.ds(pl.multiple_of(core * 64 + x * 16, 16), 16)
    antipode = device_at(x, zl, core, 1 - zh, y)
    send(kin, away_k, a_send.at[0], a_recv.at[0], antipode)
    send(pw.at[:, piece, :], away_w, a_send.at[1], a_recv.at[1], antipode)
    near_slot = zh * 2 + y % 2
    far_slot = (1 - zh) * 2 + y % 2
    not_home = jnp.logical_not(at_home)

    def spread_taps(src, slot, base):
        for k in range(8):
            target = device_at(plane, zl, core, zh, (y + k) % 8)
            if k == 0:
                here = pltpu.make_async_copy(src, taps.at[slot], k_recv.at[slot])

                @pl.when(at_home)
                def _(here=here):
                    here.start()
            else:
                copy = remote(src, taps.at[slot], k_send.at[base + k], k_recv.at[slot], target)

                @pl.when(at_home)
                def _(copy=copy):
                    copy.start()

                sent.append((at_home, copy))

    def spread_weights(src, slot, base):
        for k in range(8):
            target = device_at(plane, zl, core, zh, (y + k) % 8)
            dst = wts.at[:, slot, core, pl.ds(pl.multiple_of(x * 16, 16), 16)]
            if k == 0:
                send_if(not_home, src, dst, w_send.at[base], w_recv, target)
            else:
                send(src, dst, w_send.at[base + k], w_recv, target)

    spread_taps(kin, near_slot, 0)
    spread_weights(pw.at[:, piece, :], near_slot, 0)
    remote(kin, away_k, a_send.at[0], a_recv.at[0], antipode).wait_recv()
    spread_taps(away_k, far_slot, 8)
    remote(pw.at[:, piece, :], away_w, a_send.at[1], a_recv.at[1], antipode).wait_recv()
    spread_weights(away_w, far_slot, 8)

    for copy in own_rows:
        copy.wait()
    for k in (1, 3, 2):
        for side in range(2):
            remote(
                rows.at[x, :, sides[side]], rows.at[(x - k + 4) % 4, :, sides[side]],
                f_send.at[side, k], f_recv.at[side, k], x_peer(k),
            ).wait_recv()
    for slot in range(4):
        local_wait(taps.at[slot], k_recv.at[slot])

    def stencils(tile):
        lanes = pl.ds(pl.multiple_of(tile * LANES, LANES), LANES)
        for r in range(4):
            value = rows[r, :, lanes].astype(F32)
            wide[r, :, lanes] = value
            for i in range(2):
                moved[r, i, 20:92, lanes] = value[72 * i : 72 * i + 72]
        weights = taps[tile].astype(F32)

        def tap(b, u, v):
            t = (u + 1) * 3 + v + 1
            return weights[b, t : t + 1]

        for r in range(4):
            pieces = []
            for i in range(2):
                for q in range(3):
                    total = None
                    for u in (-1, 0, 1):
                        if not 0 <= r + u < 4:
                            continue
                        term = (
                            tap(0, u, 0) * wide[r + u, 72 * i + 24 * q : 72 * i + 24 * q + 24, lanes]
                            + tap(0, u, -1) * moved[r + u, i, 24 * q + 8 : 24 * q + 32, lanes]
                            + tap(0, u, 1) * moved[r + u, i, 24 * q + 32 : 24 * q + 56, lanes]
                        )
                        total = term if total is None else total + term
                    pieces.append(total)
            dcv[0, r, :, lanes] = jnp.concatenate(pieces, axis=0).astype(BF16)
            pieces = []
            for i in range(2):
                for q in range(3):
                    total = None
                    for u in (-1, 0, 1):
                        if not 0 <= r + 2 * u < 4:
                            continue
                        for v in (-1, 0, 1):
                            if not 0 <= q + v < 3:
                                continue
                            start = 72 * i + 24 * (q + v)
                            term = tap(1, u, v) * wide[r + 2 * u, start : start + 24, lanes]
                            total = term if total is None else total + term
                    pieces.append(total)
            dcv[1, r, :, lanes] = jnp.concatenate(pieces, axis=0).astype(BF16)

    pl.loop(0, 2)(stencils)
    local_wait(wts.at[:, :, core], w_recv)
    send(wts.at[:, :, core], wts.at[:, :, core], wc_send, wc_recv, mate)
    pl.loop(2, 4)(stencils)
    remote(
        wts.at[:, :, core], wts.at[:, :, 1 - core], wc_send, wc_recv, mate
    ).wait_recv()

    for k in (2, 1, 3, 0):
        r = (x + k) % 4
        for b in range(2):
            part = jnp.dot(
                dcv[b, r], wts[b].reshape(PART, CO), preferred_element_type=F32
            )
            if k:
                send_pre[k, :, b * CO : (b + 1) * CO] = part.astype(BF16)
            else:
                own_pre[:, b * CO : (b + 1) * CO] = part
        if k:
            send(send_pre.at[k], got_pre.at[k], p_send.at[k], p_recv.at[k], x_peer(k))
    for k in (1, 3, 2):
        remote(send_pre.at[k], got_pre.at[k], p_send.at[k], p_recv.at[k], x_peer(k)).wait_recv()
    for b in range(2):
        cols = slice(b * CO, (b + 1) * CO)
        pre = own_pre[:, cols]
        for k in (1, 3, 2):
            pre = pre + got_pre[k, :, cols].astype(F32)
        sig = 1.0 / (1.0 + jnp.exp(-pre))
        gpre[x, :, cols] = (
            cot[:, cols].astype(F32) * sig * (1.0 + pre * (1.0 - sig))
        ).astype(BF16)
        out[:, cols] = (pre * sig).astype(BF16)
    for k in (2, 1, 3):
        send(gpre.at[x], gpre.at[x], g_send.at[k], g_recv.at[k], x_peer(k))
    for k in (1, 3, 2):
        remote(
            gpre.at[x], gpre.at[(x - k + 4) % 4], g_send.at[k], g_recv.at[k], x_peer(k)
        ).wait_recv()

    @pl.loop(0, 4)
    def _(tile):
        lanes = pl.ds(pl.multiple_of(tile * LANES, LANES), LANES)
        for b in range(2):
            grad = lax.dot_general(
                dcv[b, :, :, lanes].reshape(4 * CELLS, LANES),
                gpre[:, :, b * CO : (b + 1) * CO].reshape(4 * CELLS, CO),
                (((0,), (0,)), ((), ())),
                preferred_element_type=F32,
            )
            for half in range(2):
                block = grad[64 * half : 64 * half + 64]
                wg_wide[half, tile, b] = block
                wg[half, tile, b] = block.astype(BF16)

    send(wg.at[1 - core], wg_core, c_send, c_recv, mate)

    @pl.loop(0, 4)
    def _(r):
        for b in range(2):
            back = lax.dot_general(
                gpre[r, :, b * CO : (b + 1) * CO],
                wts[b].reshape(PART, CO),
                (((1,), (1,)), ((), ())),
                preferred_element_type=F32,
            )
            if b:
                gb[r] = back
            else:
                ga[r] = back
                for i in range(2):
                    ga_moved[r, i, 20:92] = back[72 * i : 72 * i + 72]

    remote(wg.at[1 - core], wg_core, c_send, c_recv, mate).wait_recv()
    for k in range(8):
        to = (y + k) % 8
        slot = to // 2
        part = pl.ds(pl.multiple_of((to % 2) * 32, 32), 32)
        for b in range(2):
            wg_y[k, b] = (
                wg_wide[core, slot, b, part] + wg_core[slot, b, part].astype(F32)
            ).astype(BF16)
        if k:
            send(
                wg_y.at[k], wg_y_got.at[k], y_send.at[k], y_recv.at[k],
                device_at(x, zl, core, zh, to),
            )

    @pl.loop(0, 4)
    def _(tile):
        lanes = pl.ds(pl.multiple_of(tile * LANES, LANES), LANES)
        for b in range(2):
            step = b + 1
            for u in (-1, 0, 1):
                sums = [None, None, None]
                for r in range(4):
                    if not 0 <= r + step * u < 4:
                        continue
                    for i in range(2):
                        for q in range(3):
                            start = 72 * i + 24 * q
                            if b:
                                grad = gb[r, start : start + 24, lanes]
                            else:
                                grad = ga[r, start : start + 24, lanes]
                            for v in (-1, 0, 1):
                                if b:
                                    if not 0 <= q + v < 3:
                                        continue
                                    source = wide[r + 2 * u, start + 24 * v : start + 24 * v + 24, lanes]
                                elif v == 0:
                                    source = wide[r + u, start : start + 24, lanes]
                                else:
                                    begin = 24 * q + 20 + 12 * v
                                    source = moved[r + u, i, begin : begin + 24, lanes]
                                term = source * grad
                                term = term[0:8] + term[8:16] + term[16:24]
                                old = sums[v + 1]
                                sums[v + 1] = term if old is None else old + term
                for v in (-1, 0, 1):
                    t = (u + 1) * 3 + v + 1
                    total = jnp.sum(sums[v + 1], axis=0, keepdims=True)
                    kg[t // 8, tile, b, t % 8 : t % 8 + 1] = total

    send(kg.at[1 - core], kg_core, kc_send, kc_recv, mate)

    def gradient(tile):
        lanes = pl.ds(pl.multiple_of(tile * LANES, LANES), LANES)
        weights = taps[tile].astype(F32)

        def tap(b, u, v):
            t = (u + 1) * 3 + v + 1
            return weights[b, t : t + 1]

        for r in range(4):
            pieces = []
            for i in range(2):
                for q in range(3):
                    total = None
                    start = 72 * i + 24 * q
                    for u in (-1, 0, 1):
                        if 0 <= r - u < 4:
                            term = (
                                tap(0, u, 0) * ga[r - u, start : start + 24, lanes]
                                + tap(0, u, 1) * ga_moved[r - u, i, 24 * q + 8 : 24 * q + 32, lanes]
                                + tap(0, u, -1) * ga_moved[r - u, i, 24 * q + 32 : 24 * q + 56, lanes]
                            )
                            total = term if total is None else total + term
                        if 0 <= r - 2 * u < 4:
                            for v in (-1, 0, 1):
                                if 0 <= q - v < 3:
                                    begin = start - 24 * v
                                    term = tap(1, u, v) * gb[r - 2 * u, begin : begin + 24, lanes]
                                    total = term if total is None else total + term
                    pieces.append(total)
            fg_send[r, :, lanes] = jnp.concatenate(pieces, axis=0).astype(BF16)

    pl.loop(0, 2)(gradient)
    remote(kg.at[1 - core], kg_core, kc_send, kc_recv, mate).wait_recv()
    for k in range(8):
        to = (y + k) % 8
        kg_y[k] = kg[core, to // 2, to % 2] + kg_core[to // 2, to % 2]
        if k:
            send(
                kg_y.at[k], kg_y_got.at[k], ky_send.at[k], ky_recv.at[k],
                device_at(x, zl, core, zh, to),
            )
    pl.loop(2, 4)(gradient)
    for k in (2, 1, 3):
        for side in range(2):
            send(
                fg_send.at[(x + k) % 4, :, sides[side]], fgrad.at[:, channels(x, side)],
                o_send.at[side, k], o_recv.at[side, k], x_peer(k),
            )
    own_grad = [
        pltpu.make_async_copy(
            fg_send.at[x, :, sides[side]], fgrad.at[:, channels(x, side)], own_sem.at[side]
        )
        for side in range(2)
    ]
    for copy in own_grad:
        copy.start()

    for k in range(1, 8):
        remote(
            wg_y.at[k], wg_y_got.at[k], y_send.at[k], y_recv.at[k], mate
        ).wait_recv()
    for b in range(2):
        total = wg_y[0, b].astype(F32)
        for k in range(1, 8):
            total = total + wg_y_got[k, b].astype(F32)
        for h in range(2):
            for lane in range(2):
                wg_z[b * 4 + h * 2 + lane] = total[
                    16 * h : 16 * h + 16, 128 * lane : 128 * lane + 128
                ].astype(BF16)
    for j in range(8):
        owner = j if j < 4 else j + 2
        send_if(
            z != owner, wg_z.at[j], wg_z_got.at[z], z_send.at[j], z_recv,
            device_at(x, owner % 6, core, owner // 6, y),
        )
    for k in range(1, 8):
        remote(
            kg_y.at[k], kg_y_got.at[k], ky_send.at[k], ky_recv.at[k], mate
        ).wait_recv()
    total = kg_y[0]
    for k in range(1, 8):
        total = total + kg_y_got[k]
    kg_z[...] = total
    send_if(
        z != 4, kg_z, kg_z_got.at[z], kz_send, kz_recv, device_at(x, 4, core, 0, y)
    )

    half = y % 2
    home_z = y // 4
    home_y = 2 * x + (y // 2) % 2
    back_sent = []

    def spread_sums(src, dst, send_sems, recv_sem):
        for n in range(24):
            to_x, to_z = n // 6, n % 6
            same = (to_x == x) & (to_z == zl) & (home_z == zh) & (home_y == y)
            copy = remote(
                src, dst, send_sems.at[n], recv_sem, device_at(to_x, to_z, core, home_z, home_y)
            )
            here = pltpu.make_async_copy(src, dst, recv_sem)

            @pl.when(jnp.logical_not(same))
            def _(copy=copy):
                copy.start()

            @pl.when(same)
            def _(here=here):
                here.start()

            back_sent.append((same, copy))

    def wait_sums():
        for same, copy in back_sent:

            @pl.when(jnp.logical_not(same))
            def _(copy=copy):
                copy.wait_send()

        back_sent.clear()

    @pl.when(zl < 4)
    def _():
        local_wait(wg_z_got, z_recv)
        total = wg_z_got[0].astype(F32)
        for n in range(1, 12):
            total = total + wg_z_got[n].astype(F32)
        wg_red[...] = (total * FACTOR).astype(BF16)
        spread_sums(wg_red, fin.at[core, half, zh * 4 + zl], b_send, b_recv)
        wait_sums()

    @pl.when(z == 4)
    def _():
        local_wait(kg_z_got, kz_recv)
        total = kg_z_got[0]
        for n in range(1, 12):
            total = total + kg_z_got[n]
        kg_red[...] = total * FACTOR
        spread_sums(kg_red, kfin.at[core, half], kb_send, kb_recv)
        wait_sums()

    local_wait(fin.at[core], b_recv)
    send(fin.at[core], fin.at[core], e_send, e_recv, mate)
    local_wait(kfin.at[core], kb_recv)
    send(kfin.at[core], kfin.at[core], ke_send, ke_recv, mate)
    remote(fin.at[core], fin.at[1 - core], e_send, e_recv, mate).wait_recv()
    remote(kfin.at[core], kfin.at[1 - core], ke_send, ke_recv, mate).wait_recv()
    for c in range(2):
        for h in range(2):
            for j in range(8):
                b, h2, lane = j // 4, (j // 2) % 2, j % 2
                first = 64 * c + 32 * h + 16 * h2
                pgrad[b, first : first + 16, 128 * lane : 128 * lane + 128] = fin[c, h, j].astype(F32)
    for b in range(2):
        kgrad[b, 0:8] = kfin[0, b]
        kgrad[b, 8:9] = kfin[1, b, 0:1]

    for copy in own_grad:
        copy.wait()
    for k in (1, 3, 2):
        for side in range(2):
            remote(
                fg_send.at[k, :, sides[side]], fgrad.at[:, channels((x - k + 4) % 4, side)],
                o_send.at[side, k], o_recv.at[side, k], x_peer(k),
            ).wait_recv()
    for cond, copy in sent:
        if cond is None:
            copy.wait_send()
        else:

            @pl.when(cond)
            def _(copy=copy):
                copy.wait_send()


def body(features, pointwise, depthwise, cotangent):
    shape = features.shape
    anywhere = pl.BlockSpec(memory_space=pl.ANY)
    vmem = pl.BlockSpec(memory_space=pltpu.VMEM)
    dma = pltpu.SemaphoreType.DMA
    out, fgrad, pgrad, kgrad = pl.pallas_call(
        kernel,
        out_shape=(
            jax.ShapeDtypeStruct((CELLS, 2 * CO), BF16),
            jax.ShapeDtypeStruct((CELLS, C), BF16),
            jax.ShapeDtypeStruct((2, LANES, CO), F32),
            jax.ShapeDtypeStruct((2, 9, LANES), F32),
        ),
        in_specs=[anywhere, anywhere, anywhere, vmem],
        out_specs=(vmem, anywhere, vmem, vmem),
        scratch_shapes=[
            pltpu.VMEM((4, CELLS, PART), BF16),
            pltpu.VMEM((4, CELLS, PART), F32),
            pltpu.VMEM((4, 2, 112, PART), F32),
            pltpu.VMEM((4, 2, 9, LANES), BF16),
            pltpu.VMEM((2, 4, CELLS, PART), BF16),
            pltpu.VMEM((2, 4, 2, 64, CO), BF16),
            pltpu.VMEM((2, 16, CO), BF16),
            pltpu.VMEM((2, 9, LANES), BF16),
            pltpu.VMEM((CELLS, 2 * CO), F32),
            pltpu.VMEM((4, CELLS, 2 * CO), BF16),
            pltpu.VMEM((4, CELLS, 2 * CO), BF16),
            pltpu.VMEM((4, CELLS, 2 * CO), BF16),
            pltpu.VMEM((4, CELLS, PART), F32),
            pltpu.VMEM((4, 2, 112, PART), F32),
            pltpu.VMEM((4, CELLS, PART), F32),
            pltpu.VMEM((4, CELLS, PART), BF16),
            pltpu.VMEM((2, 4, 2, 64, CO), F32),
            pltpu.VMEM((2, 4, 2, 64, CO), BF16),
            pltpu.VMEM((4, 2, 64, CO), BF16),
            pltpu.VMEM((8, 2, 32, CO), BF16),
            pltpu.VMEM((8, 2, 32, CO), BF16),
            pltpu.VMEM((8, 16, LANES), BF16),
            pltpu.VMEM((12, 16, LANES), BF16),
            pltpu.VMEM((16, LANES), BF16),
            pltpu.VMEM((2, 4, 2, 8, LANES), F32),
            pltpu.VMEM((4, 2, 8, LANES), F32),
            pltpu.VMEM((8, 8, LANES), F32),
            pltpu.VMEM((8, 8, LANES), F32),
            pltpu.VMEM((8, LANES), F32),
            pltpu.VMEM((12, 8, LANES), F32),
            pltpu.VMEM((8, LANES), F32),
            pltpu.VMEM((2, 2, 8, 16, LANES), BF16),
            pltpu.VMEM((2, 2, 8, LANES), F32),
            dma((2, 4)), dma((2, 4)), dma((2,)),
            dma((2,)), dma((2,)),
            dma((16,)), dma(()),
            dma((16,)), dma((4,)),
            dma(()), dma(()),
            dma((4,)), dma((4,)),
            dma((4,)), dma((4,)),
            dma((2, 4)), dma((2, 4)),
            dma(()), dma(()),
            dma((8,)), dma((8,)),
            dma((8,)), dma(()),
            dma((24,)), dma(()),
            dma(()), dma(()),
            dma(()), dma(()),
            dma((8,)), dma((8,)),
            dma(()), dma(()),
            dma((24,)), dma(()),
            dma(()), dma(()),
        ],
        compiler_params=pltpu.CompilerParams(
            collective_id=0, has_side_effects=True, vmem_limit_bytes=40 * 1024 * 1024
        ),
    )(
        features.reshape(CELLS, C), pointwise, depthwise, cotangent.reshape(CELLS, 2 * CO)
    )
    return (
        out.reshape(*shape[:3], 2 * CO), fgrad.reshape(shape), pgrad, kgrad
    )


def solution(mesh):
    return jax.shard_map(
        body,
        mesh=mesh,
        in_specs=(
            P("dp", "space", None, None),
            P(None, "dp", None),
            P(None, None, "dp"),
            P("dp", "space", None, None),
        ),
        out_specs=(
            P("dp", "space", None, None),
            P("dp", "space", None, None),
            P(None, "dp", None),
            P(None, None, "dp"),
        ),
        check_vma=False,
    )
```

```python
import jax
import jax.numpy as jnp
from jax import lax
from jax.experimental import pallas as pl
from jax.experimental.pallas import tpu as pltpu
from jax.sharding import PartitionSpec as P

C = 2048
CO = 256
CELLS = 144
LANES = 128
PART = 512
BF16 = jnp.bfloat16
F32 = jnp.float32
MESH = pl.DeviceIdType.MESH
FACTOR = 1.0 / (110592.0**0.5)


def device_at(x, z_low, core, z_high, y):
    return {"space": (x * 6 + z_low) * 2 + core, "dp": z_high * 8 + y}


def local_wait(ref, sem):
    pltpu.make_async_copy(ref, ref, sem).wait()


def kernel(
    feat, pw, kin, cot,
    out, fgrad, pgrad, kgrad,
    rows, wide, moved, taps, dcv, wts, away_w, away_k,
    own_pre, send_pre, got_pre, gpre, ga, ga_moved, gb, fg_send,
    wg_wide, wg, wg_core, wg_y, wg_y_got, wg_z, wg_z_got, wg_red,
    kg, kg_core, kg_y, kg_y_got, kg_z, kg_z_got, kg_red, fin, kfin,
    f_send, f_recv, own_sem, a_send, a_recv, w_send, w_recv, k_send, k_recv, wc_send, wc_recv,
    p_send, p_recv, g_send, g_recv, o_send, o_recv,
    c_send, c_recv, y_send, y_recv, z_send, z_recv, b_send, b_recv, e_send, e_recv,
    kc_send, kc_recv, ky_send, ky_recv, kz_send, kz_recv, kb_send, kb_recv, ke_send, ke_recv,
):
    space = lax.axis_index("space")
    dp = lax.axis_index("dp")
    x = space // 12
    zl = (space // 2) % 6
    core = space % 2
    zh = dp // 8
    y = dp % 8
    z = zh * 6 + zl
    plane = y // 2
    at_home = x == plane
    mate = device_at(x, zl, 1 - core, zh, y)
    sent = []

    def remote(src, dst, send_sem, recv_sem, target):
        return pltpu.make_async_remote_copy(
            src_ref=src, dst_ref=dst, send_sem=send_sem, recv_sem=recv_sem,
            device_id=target, device_id_type=MESH,
        )

    def send(src, dst, send_sem, recv_sem, target):
        copy = remote(src, dst, send_sem, recv_sem, target)
        copy.start()
        sent.append((None, copy))

    def send_if(cond, src, dst, send_sem, recv_sem, target):
        copy = remote(src, dst, send_sem, recv_sem, target)
        here = pltpu.make_async_copy(src, dst, recv_sem)

        @pl.when(cond)
        def _():
            copy.start()

        @pl.when(jnp.logical_not(cond))
        def _():
            here.start()

        sent.append((cond, copy))

    def finish():
        for cond, copy in sent:
            if cond is None:
                copy.wait_send()
            else:

                @pl.when(cond)
                def _(copy=copy):
                    copy.wait_send()

    def x_peer(k):
        return device_at((x + k) % 4, zl, core, zh, y)

    def z_peer(k):
        other = (z + k) % 12
        return device_at(x, other % 6, core, other // 6, y)

    sides = (slice(0, 256), slice(256, 512))

    def channels(of_x, side):
        return pl.ds(pl.multiple_of(side * 1024 + of_x * 256, 256), 256)

    barrier = pltpu.get_barrier_semaphore()

    def greet(target):
        pl.semaphore_signal(barrier, inc=1, device_id=target, device_id_type=MESH)

    count = 0
    for k in (1, 3, 2):
        greet(x_peer(k))
        count += 1
    greet(mate)
    count += 1
    for k in range(1, 12):
        greet(z_peer(k))
        count += 1
    for k in range(1, 8):
        greet(device_at(plane, zl, core, zh, (y + k) % 8))
        count += 1
    for other in range(4):
        for near in range(2):
            target_y = 2 * x + near
            same = jnp.logical_and(other == x, target_y == y)

            @pl.when(jnp.logical_not(same))
            def _(other=other, target_y=target_y):
                greet(device_at(other, zl, core, zh, target_y))

    @pl.when(jnp.logical_not(at_home))
    def _():
        greet(device_at(plane, zl, core, zh, y))

    count += 9
    moved[...] = jnp.zeros_like(moved)
    ga_moved[...] = jnp.zeros_like(ga_moved)
    kg[...] = jnp.zeros_like(kg)
    pl.semaphore_wait(barrier, count - 2 * at_home.astype(jnp.int32))

    for side in range(2):
        for k in (2, 1, 3):
            send(
                feat.at[:, channels((x + k) % 4, side)], rows.at[x, :, sides[side]],
                f_send.at[side, k], f_recv.at[side, k], x_peer(k),
            )
    own_rows = [
        pltpu.make_async_copy(
            feat.at[:, channels(x, side)], rows.at[x, :, sides[side]], own_sem.at[side]
        )
        for side in range(2)
    ]
    for copy in own_rows:
        copy.start()

    piece = pl.ds(pl.multiple_of(core * 64 + x * 16, 16), 16)
    partner = device_at(x, (zl + 3) % 6, core, 1 - zh, y)
    send(kin, away_k, a_send.at[0], a_recv.at[0], partner)
    send(pw.at[:, piece, :], away_w, a_send.at[1], a_recv.at[1], partner)
    near_slot = zh * 2 + y % 2
    far_slot = (1 - zh) * 2 + y % 2
    not_home = jnp.logical_not(at_home)

    def spread_taps(src, slot, base):
        for k in range(8):
            target = device_at(plane, zl, core, zh, (y + k) % 8)
            if k == 0:
                here = pltpu.make_async_copy(src, taps.at[slot], k_recv.at[slot])

                @pl.when(at_home)
                def _(here=here):
                    here.start()
            else:
                copy = remote(src, taps.at[slot], k_send.at[base + k], k_recv.at[slot], target)

                @pl.when(at_home)
                def _(copy=copy):
                    copy.start()

                sent.append((at_home, copy))

    def spread_weights(src, slot, base):
        for k in range(8):
            target = device_at(plane, zl, core, zh, (y + k) % 8)
            dst = wts.at[:, slot, core, pl.ds(pl.multiple_of(x * 16, 16), 16)]
            if k == 0:
                send_if(not_home, src, dst, w_send.at[base], w_recv, target)
            else:
                send(src, dst, w_send.at[base + k], w_recv, target)

    spread_taps(kin, near_slot, 0)
    spread_weights(pw.at[:, piece, :], near_slot, 0)
    remote(kin, away_k, a_send.at[0], a_recv.at[0], partner).wait_recv()
    spread_taps(away_k, far_slot, 8)
    remote(pw.at[:, piece, :], away_w, a_send.at[1], a_recv.at[1], partner).wait_recv()
    spread_weights(away_w, far_slot, 8)

    def tap_of(tile):
        weights = taps[tile].astype(F32)

        def tap(b, u, v):
            t = (u + 1) * 3 + v + 1
            return weights[t, b : b + 1]

        return tap

    def lanes_of(tile):
        return pl.ds(pl.multiple_of(tile * LANES, LANES), LANES)

    def stencils_a(tile):
        lanes = lanes_of(tile)
        for r in range(4):
            value = rows[r, :, lanes].astype(F32)
            wide[r, :, lanes] = value
            for i in range(2):
                moved[r, i, 20:92, lanes] = value[72 * i : 72 * i + 72]
        tap = tap_of(tile)
        for r in range(4):
            pieces = []
            for i in range(2):
                for q in range(3):
                    total = None
                    for u in (-1, 0, 1):
                        if not 0 <= r + u < 4:
                            continue
                        term = (
                            tap(0, u, 0) * wide[r + u, 72 * i + 24 * q : 72 * i + 24 * q + 24, lanes]
                            + tap(0, u, -1) * moved[r + u, i, 24 * q + 8 : 24 * q + 32, lanes]
                            + tap(0, u, 1) * moved[r + u, i, 24 * q + 32 : 24 * q + 56, lanes]
                        )
                        total = term if total is None else total + term
                    pieces.append(total)
            dcv[0, r, :, lanes] = jnp.concatenate(pieces, axis=0).astype(BF16)

    def stencils_b(tile):
        lanes = lanes_of(tile)
        tap = tap_of(tile)
        for r in range(4):
            pieces = []
            for i in range(2):
                for q in range(3):
                    total = None
                    for u in (-1, 0, 1):
                        if not 0 <= r + 2 * u < 4:
                            continue
                        for v in (-1, 0, 1):
                            if not 0 <= q + v < 3:
                                continue
                            start = 72 * i + 24 * (q + v)
                            term = tap(1, u, v) * wide[r + 2 * u, start : start + 24, lanes]
                            total = term if total is None else total + term
                    pieces.append(total)
            dcv[1, r, :, lanes] = jnp.concatenate(pieces, axis=0).astype(BF16)

    for slot in range(4):
        local_wait(taps.at[slot], k_recv.at[slot])
    for side in range(2):
        own_rows[side].wait()
        for k in (1, 3, 2):
            remote(
                rows.at[x, :, sides[side]], rows.at[(x - k + 4) % 4, :, sides[side]],
                f_send.at[side, k], f_recv.at[side, k], x_peer(k),
            ).wait_recv()
        pl.loop(2 * side, 2 * side + 2)(stencils_a)

    local_wait(wts.at[:, :, core], w_recv)
    send(wts.at[:, :, core], wts.at[:, :, core], wc_send, wc_recv, mate)
    pl.loop(0, 2)(stencils_b)
    remote(
        wts.at[:, :, core], wts.at[:, :, 1 - core], wc_send, wc_recv, mate
    ).wait_recv()

    def products(b):
        for k in (2, 1, 3, 0):
            part = jnp.dot(
                dcv[b, (x + k) % 4], wts[b].reshape(PART, CO), preferred_element_type=F32
            )
            if k:
                send_pre[b, k] = part.astype(BF16)
                send(send_pre.at[b, k], got_pre.at[b, k], p_send.at[b, k], p_recv.at[b, k], x_peer(k))
            else:
                own_pre[b] = part

    products(0)
    pl.loop(2, 4)(stencils_b)
    products(1)
    for b in range(2):
        cols = slice(b * CO, (b + 1) * CO)
        for k in (1, 3, 2):
            remote(
                send_pre.at[b, k], got_pre.at[b, k], p_send.at[b, k], p_recv.at[b, k], x_peer(k)
            ).wait_recv()
        pre = own_pre[b]
        for k in (1, 3, 2):
            pre = pre + got_pre[b, k].astype(F32)
        sig = 1.0 / (1.0 + jnp.exp(-pre))
        gpre[b, x] = (cot[:, cols].astype(F32) * sig * (1.0 + pre * (1.0 - sig))).astype(BF16)
        for k in (2, 1, 3):
            send(gpre.at[b, x], gpre.at[b, x], g_send.at[b, k], g_recv.at[b, k], x_peer(k))
        out[:, cols] = (pre * sig).astype(BF16)

    def wait_gpre(b):
        for k in (1, 3, 2):
            remote(
                gpre.at[b, x], gpre.at[b, (x - k + 4) % 4], g_send.at[b, k], g_recv.at[b, k], x_peer(k)
            ).wait_recv()

    def weight_gradient(b):
        @pl.loop(0, 4)
        def _(tile):
            grad = lax.dot_general(
                dcv[b, :, :, lanes_of(tile)].reshape(4 * CELLS, LANES),
                gpre[b].reshape(4 * CELLS, CO),
                (((0,), (0,)), ((), ())),
                preferred_element_type=F32,
            )
            for half in range(2):
                block = grad[64 * half : 64 * half + 64]
                wg_wide[b, half, tile] = block
                wg[b, half, tile] = block.astype(BF16)

        send(wg.at[b, 1 - core], wg_core.at[b], c_send.at[b], c_recv.at[b], mate)

    def stencil_gradient(b):
        @pl.loop(0, 4)
        def _(r):
            back = lax.dot_general(
                gpre[b, r], wts[b].reshape(PART, CO), (((1,), (1,)), ((), ())),
                preferred_element_type=F32,
            )
            if b:
                gb[r] = back
            else:
                ga[r] = back
                for i in range(2):
                    ga_moved[r, i, 20:92] = back[72 * i : 72 * i + 72]

    def sum_over_y(b):
        remote(
            wg.at[b, 1 - core], wg_core.at[b], c_send.at[b], c_recv.at[b], mate
        ).wait_recv()
        for k in (4, 3, 5, 2, 6, 1, 7, 0):
            to = (y + k) % 8
            slot = to // 2
            part = pl.ds(pl.multiple_of((to % 2) * 32, 32), 32)
            wg_y[b, k] = (
                wg_wide[b, core, slot, part] + wg_core[b, slot, part].astype(F32)
            ).astype(BF16)
            if k:
                send(
                    wg_y.at[b, k], wg_y_got.at[b, k], y_send.at[b, k], y_recv.at[b, k],
                    device_at(x, zl, core, zh, to),
                )

    def tap_gradient(b):
        step = b + 1

        @pl.loop(0, 4)
        def _(tile):
            lanes = lanes_of(tile)
            for u in (-1, 0, 1):
                sums = [None, None, None]
                for r in range(4):
                    if not 0 <= r + step * u < 4:
                        continue
                    for i in range(2):
                        for q in range(3):
                            start = 72 * i + 24 * q
                            if b:
                                grad = gb[r, start : start + 24, lanes]
                            else:
                                grad = ga[r, start : start + 24, lanes]
                            for v in (-1, 0, 1):
                                if b:
                                    if not 0 <= q + v < 3:
                                        continue
                                    source = wide[r + 2 * u, start + 24 * v : start + 24 * v + 24, lanes]
                                elif v == 0:
                                    source = wide[r + u, start : start + 24, lanes]
                                else:
                                    begin = 24 * q + 20 + 12 * v
                                    source = moved[r + u, i, begin : begin + 24, lanes]
                                term = source * grad
                                term = term[0:8] + term[8:16] + term[16:24]
                                old = sums[v + 1]
                                sums[v + 1] = term if old is None else old + term
                for v in (-1, 0, 1):
                    t = (u + 1) * 3 + v + 1
                    total = jnp.sum(sums[v + 1], axis=0, keepdims=True)
                    kg[t // 8, tile, b, t % 8 : t % 8 + 1] = total

    wait_gpre(0)
    weight_gradient(0)
    stencil_gradient(0)
    sum_over_y(0)
    tap_gradient(0)
    wait_gpre(1)
    weight_gradient(1)
    stencil_gradient(1)
    sum_over_y(1)
    tap_gradient(1)
    send(kg.at[1 - core], kg_core, kc_send, kc_recv, mate)

    def gradient(tile):
        lanes = lanes_of(tile)
        tap = tap_of(tile)
        for r in range(4):
            pieces = []
            for i in range(2):
                for q in range(3):
                    total = None
                    start = 72 * i + 24 * q
                    for u in (-1, 0, 1):
                        if 0 <= r - u < 4:
                            term = (
                                tap(0, u, 0) * ga[r - u, start : start + 24, lanes]
                                + tap(0, u, 1) * ga_moved[r - u, i, 24 * q + 8 : 24 * q + 32, lanes]
                                + tap(0, u, -1) * ga_moved[r - u, i, 24 * q + 32 : 24 * q + 56, lanes]
                            )
                            total = term if total is None else total + term
                        if 0 <= r - 2 * u < 4:
                            for v in (-1, 0, 1):
                                if 0 <= q - v < 3:
                                    begin = start - 24 * v
                                    term = tap(1, u, v) * gb[r - 2 * u, begin : begin + 24, lanes]
                                    total = term if total is None else total + term
                    pieces.append(total)
            fg_send[r, :, lanes] = jnp.concatenate(pieces, axis=0).astype(BF16)

    pl.loop(0, 2)(gradient)
    remote(kg.at[1 - core], kg_core, kc_send, kc_recv, mate).wait_recv()
    for k in range(8):
        to = (y + k) % 8
        kg_y[k] = kg[core, to // 2, to % 2] + kg_core[to // 2, to % 2]
        if k:
            send(
                kg_y.at[k], kg_y_got.at[k], ky_send.at[k], ky_recv.at[k],
                device_at(x, zl, core, zh, to),
            )
    home_z = y // 4
    home_y = 2 * x + (y // 2) % 2
    for b in range(2):
        for k in range(1, 8):
            remote(
                wg_y.at[b, k], wg_y_got.at[b, k], y_send.at[b, k], y_recv.at[b, k], mate
            ).wait_recv()
        total = wg_y[b, 0].astype(F32)
        for k in range(1, 8):
            total = total + wg_y_got[b, k].astype(F32)
        for h in range(2):
            wg_z[2 * b + h] = total[16 * h : 16 * h + 16].astype(BF16)
            send_if(
                jnp.logical_or(zl != 1 + 2 * b + h, zh != home_z),
                wg_z.at[2 * b + h], wg_z_got.at[z], z_send.at[2 * b + h], z_recv,
                device_at(x, 1 + 2 * b + h, core, home_z, y),
            )
    pl.loop(2, 4)(gradient)
    for side in range(2):
        for k in (2, 1, 3):
            send(
                fg_send.at[(x + k) % 4, :, sides[side]], fgrad.at[:, channels(x, side)],
                o_send.at[side, k], o_recv.at[side, k], x_peer(k),
            )
    own_grad = [
        pltpu.make_async_copy(
            fg_send.at[x, :, sides[side]], fgrad.at[:, channels(x, side)], own_sem.at[side]
        )
        for side in range(2)
    ]
    for copy in own_grad:
        copy.start()
    for k in range(1, 8):
        remote(
            kg_y.at[k], kg_y_got.at[k], ky_send.at[k], ky_recv.at[k], mate
        ).wait_recv()
    total = kg_y[0]
    for k in range(1, 8):
        total = total + kg_y_got[k]
    kg_z[...] = total
    send_if(
        jnp.logical_or(zl != 5, zh != home_z),
        kg_z, kg_z_got.at[z], kz_send, kz_recv, device_at(x, 5, core, home_z, y),
    )

    half = y % 2
    back_sent = []

    def spread_sums(src, dst, send_sems, recv_sem):
        for n in range(24):
            to_x, to_z = n // 6, n % 6
            same = (to_x == x) & (to_z == zl) & (home_z == zh) & (home_y == y)
            copy = remote(
                src, dst, send_sems.at[n], recv_sem, device_at(to_x, to_z, core, home_z, home_y)
            )
            here = pltpu.make_async_copy(src, dst, recv_sem)

            @pl.when(jnp.logical_not(same))
            def _(copy=copy):
                copy.start()

            @pl.when(same)
            def _(here=here):
                here.start()

            back_sent.append((same, copy))

    def wait_sums():
        for same, copy in back_sent:

            @pl.when(jnp.logical_not(same))
            def _(copy=copy):
                copy.wait_send()

        back_sent.clear()

    @pl.when((zh == home_z) & (zl > 0) & (zl < 5))
    def _():
        local_wait(wg_z_got, z_recv)
        total = wg_z_got[0].astype(F32)
        for n in range(1, 12):
            total = total + wg_z_got[n].astype(F32)
        wg_red[...] = (total * FACTOR).astype(BF16)
        spread_sums(wg_red, fin.at[core, half, zl - 1], b_send, b_recv)
        wait_sums()

    @pl.when((zh == home_z) & (zl == 5))
    def _():
        local_wait(kg_z_got, kz_recv)
        total = kg_z_got[0]
        for n in range(1, 12):
            total = total + kg_z_got[n]
        kg_red[...] = total * FACTOR
        spread_sums(kg_red, kfin.at[core, half], kb_send, kb_recv)
        wait_sums()

    local_wait(fin.at[core], b_recv)
    send(fin.at[core], fin.at[core], e_send, e_recv, mate)
    local_wait(kfin.at[core], kb_recv)
    send(kfin.at[core], kfin.at[core], ke_send, ke_recv, mate)
    remote(fin.at[core], fin.at[1 - core], e_send, e_recv, mate).wait_recv()
    remote(kfin.at[core], kfin.at[1 - core], ke_send, ke_recv, mate).wait_recv()
    for c in range(2):
        for h in range(2):
            for j in range(4):
                first = 64 * c + 32 * h + 16 * (j % 2)
                pgrad[j // 2, first : first + 16] = fin[c, h, j].astype(F32)
    for b in range(2):
        for t in range(9):
            kgrad[t, b : b + 1] = kfin[t // 8, b, t % 8 : t % 8 + 1]

    for copy in own_grad:
        copy.wait()
    for k in (1, 3, 2):
        for side in range(2):
            remote(
                fg_send.at[k, :, sides[side]], fgrad.at[:, channels((x - k + 4) % 4, side)],
                o_send.at[side, k], o_recv.at[side, k], x_peer(k),
            ).wait_recv()
    finish()


def hand_over(*refs):
    arrays, results, sems = refs[:4], refs[4:8], refs[8]
    copies = [
        pltpu.make_async_copy(array, result, sems.at[n])
        for n, (array, result) in enumerate(zip(arrays, results))
    ]
    for copy in copies:
        copy.start()
    for copy in copies:
        copy.wait()


def body(features, pointwise, depthwise, cotangent):
    shape = features.shape
    anywhere = pl.BlockSpec(memory_space=pl.ANY)
    vmem = pl.BlockSpec(memory_space=pltpu.VMEM)
    dma = pltpu.SemaphoreType.DMA
    out, fgrad, pgrad, kgrad = pl.pallas_call(
        kernel,
        out_shape=(
            pltpu.VMEM((CELLS, 2 * CO), BF16),
            pltpu.VMEM((CELLS, C), BF16),
            pltpu.VMEM((2, LANES, CO), F32),
            pltpu.VMEM((9, 2, LANES), F32),
        ),
        in_specs=[anywhere, anywhere, anywhere, vmem],
        out_specs=(vmem, vmem, vmem, vmem),
        scratch_shapes=[
            pltpu.VMEM((4, CELLS, PART), BF16),
            pltpu.VMEM((4, CELLS, PART), F32),
            pltpu.VMEM((4, 2, 112, PART), F32),
            pltpu.VMEM((4, 9, 2, LANES), BF16),
            pltpu.VMEM((2, 4, CELLS, PART), BF16),
            pltpu.VMEM((2, 4, 2, 64, CO), BF16),
            pltpu.VMEM((2, 16, CO), BF16),
            pltpu.VMEM((9, 2, LANES), BF16),
            pltpu.VMEM((2, CELLS, CO), F32),
            pltpu.VMEM((2, 4, CELLS, CO), BF16),
            pltpu.VMEM((2, 4, CELLS, CO), BF16),
            pltpu.VMEM((2, 4, CELLS, CO), BF16),
            pltpu.VMEM((4, CELLS, PART), F32),
            pltpu.VMEM((4, 2, 112, PART), F32),
            pltpu.VMEM((4, CELLS, PART), F32),
            pltpu.VMEM((4, CELLS, PART), BF16),
            pltpu.VMEM((2, 2, 4, 64, CO), F32),
            pltpu.VMEM((2, 2, 4, 64, CO), BF16),
            pltpu.VMEM((2, 4, 64, CO), BF16),
            pltpu.VMEM((2, 8, 32, CO), BF16),
            pltpu.VMEM((2, 8, 32, CO), BF16),
            pltpu.VMEM((4, 16, CO), BF16),
            pltpu.VMEM((12, 16, CO), BF16),
            pltpu.VMEM((16, CO), BF16),
            pltpu.VMEM((2, 4, 2, 8, LANES), F32),
            pltpu.VMEM((4, 2, 8, LANES), F32),
            pltpu.VMEM((8, 8, LANES), F32),
            pltpu.VMEM((8, 8, LANES), F32),
            pltpu.VMEM((8, LANES), F32),
            pltpu.VMEM((12, 8, LANES), F32),
            pltpu.VMEM((8, LANES), F32),
            pltpu.VMEM((2, 2, 4, 16, CO), BF16),
            pltpu.VMEM((2, 2, 8, LANES), F32),
            dma((2, 4)), dma((2, 4)), dma((2,)),
            dma((2,)), dma((2,)),
            dma((16,)), dma(()),
            dma((16,)), dma((4,)),
            dma(()), dma(()),
            dma((2, 4)), dma((2, 4)),
            dma((2, 4)), dma((2, 4)),
            dma((2, 4)), dma((2, 4)),
            dma((2,)), dma((2,)),
            dma((2, 8)), dma((2, 8)),
            dma((4,)), dma(()),
            dma((24,)), dma(()),
            dma(()), dma(()),
            dma(()), dma(()),
            dma((8,)), dma((8,)),
            dma(()), dma(()),
            dma((24,)), dma(()),
            dma(()), dma(()),
        ],
        compiler_params=pltpu.CompilerParams(
            collective_id=0, has_side_effects=True, vmem_limit_bytes=60 * 1024 * 1024
        ),
    )(
        features.reshape(CELLS, C), pointwise, depthwise.transpose(1, 0, 2), cotangent.reshape(CELLS, 2 * CO)
    )
    made = (out, fgrad, pgrad, kgrad)
    out, fgrad, pgrad, kgrad = pl.pallas_call(
        hand_over,
        out_shape=tuple(jax.ShapeDtypeStruct(m.shape, m.dtype) for m in made),
        in_specs=[anywhere] * 4,
        out_specs=(anywhere,) * 4,
        scratch_shapes=[dma((4,))],
        compiler_params=pltpu.CompilerParams(vmem_limit_bytes=1024 * 1024),
    )(*made)
    return (
        out.reshape(*shape[:3], 2 * CO), fgrad.reshape(shape), pgrad, kgrad.transpose(1, 0, 2)
    )


def solution(mesh):
    return jax.shard_map(
        body,
        mesh=mesh,
        in_specs=(
            P("dp", "space", None, None),
            P(None, "dp", None),
            P(None, None, "dp"),
            P("dp", "space", None, None),
        ),
        out_specs=(
            P("dp", "space", None, None),
            P("dp", "space", None, None),
            P(None, "dp", None),
            P(None, None, "dp"),
        ),
        check_vma=False,
    )
```

```python
import jax
import jax.numpy as jnp
from jax import lax
from jax.experimental import pallas as pl
from jax.experimental.pallas import tpu as pltpu
from jax.sharding import PartitionSpec as P

C = 2048
CO = 256
CELLS = 144
LANES = 128
PART = 512
BF16 = jnp.bfloat16
F32 = jnp.float32
MESH = pl.DeviceIdType.MESH
FACTOR = 1.0 / (110592.0**0.5)


def device_at(x, z_low, core, z_high, y):
    return {"space": (x * 6 + z_low) * 2 + core, "dp": z_high * 8 + y}


def local_wait(ref, sem):
    pltpu.make_async_copy(ref, ref, sem).wait()


def kernel(
    feat, pw, kin, cot,
    out, fgrad, pgrad, kgrad,
    rows, cot_here, wide, moved, taps, dcv, wts, away_w, away_k,
    own_pre, send_pre, got_pre, gpre, ga, ga_moved, gb, fg_send,
    wg_wide, wg, wg_core, wg_y, wg_y_got, wg_z, wg_z_got, wg_red,
    kg, kg_got, kg_z, kg_z_got, kg_red, mid, kmid, fin, kfin,
    f_send, f_recv, own_sem, cot_sem, a_send, a_recv, w_send, w_recv, k_send, k_recv, wc_send, wc_recv,
    p_send, p_recv, g_send, g_recv, o_send, o_recv,
    c_send, c_recv, y_send, y_recv, z_send, z_recv, b_send, b_recv, d_send, d_recv, e_send, e_recv,
    ky_send, ky_recv, kz_send, kz_recv, kb_send, kb_recv, kd_send, kd_recv, ke_send, ke_recv,
):
    space = lax.axis_index("space")
    dp = lax.axis_index("dp")
    x = space // 12
    zl = (space // 2) % 6
    core = space % 2
    zh = dp // 8
    y = dp % 8
    z = zh * 6 + zl
    plane = y // 2
    at_home = x == plane
    mate = device_at(x, zl, 1 - core, zh, y)
    sent = []

    def remote(src, dst, send_sem, recv_sem, target):
        return pltpu.make_async_remote_copy(
            src_ref=src, dst_ref=dst, send_sem=send_sem, recv_sem=recv_sem,
            device_id=target, device_id_type=MESH,
        )

    def send(src, dst, send_sem, recv_sem, target):
        copy = remote(src, dst, send_sem, recv_sem, target)
        copy.start()
        sent.append((None, copy))

    def send_if(cond, src, dst, send_sem, recv_sem, target):
        copy = remote(src, dst, send_sem, recv_sem, target)
        here = pltpu.make_async_copy(src, dst, recv_sem)

        @pl.when(cond)
        def _():
            copy.start()

        @pl.when(jnp.logical_not(cond))
        def _():
            here.start()

        sent.append((cond, copy))

    def finish():
        for cond, copy in sent:
            if cond is None:
                copy.wait_send()
            else:

                @pl.when(cond)
                def _(copy=copy):
                    copy.wait_send()

    def x_peer(k):
        return device_at((x + k) % 4, zl, core, zh, y)

    def z_peer(k):
        other = (z + k) % 12
        return device_at(x, other % 6, core, other // 6, y)

    sides = (slice(0, 256), slice(256, 512))

    def channels(of_x, side):
        return pl.ds(pl.multiple_of(side * 1024 + of_x * 256, 256), 256)

    barrier = pltpu.get_barrier_semaphore()

    def greet(target):
        pl.semaphore_signal(barrier, inc=1, device_id=target, device_id_type=MESH)

    count = 0
    for k in (1, 3, 2):
        greet(x_peer(k))
        count += 1
    greet(mate)
    count += 1
    for k in range(1, 12):
        greet(z_peer(k))
        count += 1
    for k in range(1, 8):
        greet(device_at(plane, zl, core, zh, (y + k) % 8))
        count += 1
    for other in range(4):
        for near in range(2):
            target_y = 2 * x + near
            same = jnp.logical_and(other == x, target_y == y)

            @pl.when(jnp.logical_not(same))
            def _(other=other, target_y=target_y):
                greet(device_at(other, zl, core, zh, target_y))

    @pl.when(jnp.logical_not(at_home))
    def _():
        greet(device_at(plane, zl, core, zh, y))

    count += 9
    pl.semaphore_wait(barrier, count - 2 * at_home.astype(jnp.int32))

    def send_rows(side):
        for k in (2, 1, 3):
            send(
                feat.at[:, channels((x + k) % 4, side)], rows.at[x, :, sides[side]],
                f_send.at[side, k], f_recv.at[side, k], x_peer(k),
            )

    piece = pl.ds(pl.multiple_of(core * 64 + x * 16, 16), 16)
    partner = device_at(x, (zl + 3) % 6, core, 1 - zh, y)
    send(kin, away_k, a_send.at[2], a_recv.at[2], partner)
    for b in range(2):
        send(pw.at[b, piece], away_w.at[b], a_send.at[b], a_recv.at[b], partner)
    near_slot = zh * 2 + y % 2
    far_slot = (1 - zh) * 2 + y % 2
    not_home = jnp.logical_not(at_home)

    def spread_taps(src, slot, base):
        for k in range(8):
            target = device_at(plane, zl, core, zh, (y + k) % 8)
            if k == 0:
                here = pltpu.make_async_copy(src, taps.at[slot], k_recv.at[slot])

                @pl.when(at_home)
                def _(here=here):
                    here.start()
            else:
                copy = remote(src, taps.at[slot], k_send.at[base + k], k_recv.at[slot], target)

                @pl.when(at_home)
                def _(copy=copy):
                    copy.start()

                sent.append((at_home, copy))

    def spread_weights(b, src, slot, base):
        for k in range(8):
            target = device_at(plane, zl, core, zh, (y + k) % 8)
            dst = wts.at[b, slot, core, pl.ds(pl.multiple_of(x * 16, 16), 16)]
            if k == 0:
                send_if(not_home, src, dst, w_send.at[base], w_recv.at[b], target)
            else:
                send(src, dst, w_send.at[base + k], w_recv.at[b], target)

    spread_taps(kin, near_slot, 0)
    for b in range(2):
        spread_weights(b, pw.at[b, piece], near_slot, 16 * b)
    send_rows(0)
    own_rows = [
        pltpu.make_async_copy(
            feat.at[:, channels(x, side)], rows.at[x, :, sides[side]], own_sem.at[side]
        )
        for side in range(2)
    ]
    for copy in own_rows:
        copy.start()
    cot_copy = pltpu.make_async_copy(cot, cot_here, cot_sem)
    cot_copy.start()
    border = jnp.zeros((24, PART), F32)
    for r in range(4):
        for i in range(2):
            for array in (moved, ga_moved):
                array[r, i, 0:24] = border
                array[r, i, 88:112] = border
    kg[...] = jnp.zeros_like(kg)
    remote(kin, away_k, a_send.at[2], a_recv.at[2], partner).wait_recv()
    spread_taps(away_k, far_slot, 8)
    for b in range(2):
        remote(pw.at[b, piece], away_w.at[b], a_send.at[b], a_recv.at[b], partner).wait_recv()
        spread_weights(b, away_w.at[b], far_slot, 16 * b + 8)
    send_rows(1)

    def tap_of(tile):
        weights = taps[tile].astype(F32)

        def tap(b, u, v):
            t = (u + 1) * 3 + v + 1
            return weights[t, b : b + 1]

        return tap

    def lanes_of(tile):
        return pl.ds(pl.multiple_of(tile * LANES, LANES), LANES)

    def stencils_a(tile):
        lanes = lanes_of(tile)
        for r in range(4):
            value = rows[r, :, lanes].astype(F32)
            wide[r, :, lanes] = value
            for i in range(2):
                moved[r, i, 20:92, lanes] = value[72 * i : 72 * i + 72]
        tap = tap_of(tile)
        for r in range(4):
            pieces = []
            for i in range(2):
                for q in range(3):
                    total = None
                    for u in (-1, 0, 1):
                        if not 0 <= r + u < 4:
                            continue
                        term = (
                            tap(0, u, 0) * wide[r + u, 72 * i + 24 * q : 72 * i + 24 * q + 24, lanes]
                            + tap(0, u, -1) * moved[r + u, i, 24 * q + 8 : 24 * q + 32, lanes]
                            + tap(0, u, 1) * moved[r + u, i, 24 * q + 32 : 24 * q + 56, lanes]
                        )
                        total = term if total is None else total + term
                    pieces.append(total)
            dcv[0, r, :, lanes] = jnp.concatenate(pieces, axis=0).astype(BF16)

    def stencils_b(tile):
        lanes = lanes_of(tile)
        tap = tap_of(tile)
        for r in range(4):
            pieces = []
            for i in range(2):
                for q in range(3):
                    total = None
                    for u in (-1, 0, 1):
                        if not 0 <= r + 2 * u < 4:
                            continue
                        for v in (-1, 0, 1):
                            if not 0 <= q + v < 3:
                                continue
                            start = 72 * i + 24 * (q + v)
                            term = tap(1, u, v) * wide[r + 2 * u, start : start + 24, lanes]
                            total = term if total is None else total + term
                    pieces.append(total)
            dcv[1, r, :, lanes] = jnp.concatenate(pieces, axis=0).astype(BF16)

    for slot in range(4):
        local_wait(taps.at[slot], k_recv.at[slot])
    for side in range(2):
        own_rows[side].wait()
        for k in (1, 3, 2):
            remote(
                rows.at[x, :, sides[side]], rows.at[(x - k + 4) % 4, :, sides[side]],
                f_send.at[side, k], f_recv.at[side, k], x_peer(k),
            ).wait_recv()
        pl.loop(2 * side, 2 * side + 2)(stencils_a)

    def trade_weights(b):
        local_wait(wts.at[b, :, core], w_recv.at[b])
        send(wts.at[b, :, core], wts.at[b, :, core], wc_send.at[b], wc_recv.at[b], mate)

    def wait_weights(b):
        remote(
            wts.at[b, :, core], wts.at[b, :, 1 - core], wc_send.at[b], wc_recv.at[b], mate
        ).wait_recv()

    trade_weights(0)
    pl.loop(0, 4)(stencils_b)
    trade_weights(1)

    def products(b):
        for k in (2, 1, 3, 0):
            part = jnp.dot(
                dcv[b, (x + k) % 4], wts[b].reshape(PART, CO), preferred_element_type=F32
            )
            if k:
                send_pre[b, k] = part.astype(BF16)
                send(send_pre.at[b, k], got_pre.at[b, k], p_send.at[b, k], p_recv.at[b, k], x_peer(k))
            else:
                own_pre[b] = part

    wait_weights(0)
    products(0)
    wait_weights(1)
    products(1)
    cot_copy.wait()
    for b in range(2):
        cols = slice(b * CO, (b + 1) * CO)
        for k in (1, 3, 2):
            remote(
                send_pre.at[b, k], got_pre.at[b, k], p_send.at[b, k], p_recv.at[b, k], x_peer(k)
            ).wait_recv()
        pre = own_pre[b]
        for k in (1, 3, 2):
            pre = pre + got_pre[b, k].astype(F32)
        sig = 1.0 / (1.0 + jnp.exp(-pre))
        gpre[b, x] = (cot_here[:, cols].astype(F32) * sig * (1.0 + pre * (1.0 - sig))).astype(BF16)
        for k in (2, 1, 3):
            send(gpre.at[b, x], gpre.at[b, x], g_send.at[b, k], g_recv.at[b, k], x_peer(k))
        out[:, cols] = (pre * sig).astype(BF16)

    def wait_gpre(b):
        for k in (1, 3, 2):
            remote(
                gpre.at[b, x], gpre.at[b, (x - k + 4) % 4], g_send.at[b, k], g_recv.at[b, k], x_peer(k)
            ).wait_recv()

    def weight_gradient(b):
        @pl.loop(0, 4)
        def _(tile):
            grad = lax.dot_general(
                dcv[b, :, :, lanes_of(tile)].reshape(4 * CELLS, LANES),
                gpre[b].reshape(4 * CELLS, CO),
                (((0,), (0,)), ((), ())),
                preferred_element_type=F32,
            )
            for half in range(2):
                block = grad[64 * half : 64 * half + 64]
                wg_wide[b, half, tile] = block
                wg[b, half, tile] = block.astype(BF16)

        send(wg.at[b, 1 - core], wg_core.at[b], c_send.at[b], c_recv.at[b], mate)

    def stencil_gradient(b):
        @pl.loop(0, 4)
        def _(r):
            back = lax.dot_general(
                gpre[b, r], wts[b].reshape(PART, CO), (((1,), (1,)), ((), ())),
                preferred_element_type=F32,
            )
            if b:
                gb[r] = back
            else:
                ga[r] = back
                for i in range(2):
                    ga_moved[r, i, 20:92] = back[72 * i : 72 * i + 72]

    def sum_over_y(b):
        remote(
            wg.at[b, 1 - core], wg_core.at[b], c_send.at[b], c_recv.at[b], mate
        ).wait_recv()
        for k in (4, 3, 5, 2, 6, 1, 7, 0):
            to = (y + k) % 8
            slot = to // 2
            part = pl.ds(pl.multiple_of((to % 2) * 32, 32), 32)
            wg_y[b, k] = (
                wg_wide[b, core, slot, part] + wg_core[b, slot, part].astype(F32)
            ).astype(BF16)
            if k:
                send(
                    wg_y.at[b, k], wg_y_got.at[b, k], y_send.at[b, k], y_recv.at[b, k],
                    device_at(x, zl, core, zh, to),
                )

    def tap_gradient(b):
        step = b + 1

        @pl.loop(0, 4)
        def _(tile):
            lanes = lanes_of(tile)
            for u in (-1, 0, 1):
                sums = [None, None, None]
                for r in range(4):
                    if not 0 <= r + step * u < 4:
                        continue
                    for i in range(2):
                        for q in range(3):
                            start = 72 * i + 24 * q
                            if b:
                                grad = gb[r, start : start + 24, lanes]
                            else:
                                grad = ga[r, start : start + 24, lanes]
                            for v in (-1, 0, 1):
                                if b:
                                    if not 0 <= q + v < 3:
                                        continue
                                    source = wide[r + 2 * u, start + 24 * v : start + 24 * v + 24, lanes]
                                elif v == 0:
                                    source = wide[r + u, start : start + 24, lanes]
                                else:
                                    begin = 24 * q + 20 + 12 * v
                                    source = moved[r + u, i, begin : begin + 24, lanes]
                                term = source * grad
                                term = term[0:8] + term[8:16] + term[16:24]
                                old = sums[v + 1]
                                sums[v + 1] = term if old is None else old + term
                for v in (-1, 0, 1):
                    t = (u + 1) * 3 + v + 1
                    total = jnp.sum(sums[v + 1], axis=0, keepdims=True)
                    kg[t // 8, tile, b, t % 8 : t % 8 + 1] = total

    wait_gpre(0)
    weight_gradient(0)
    stencil_gradient(0)
    sum_over_y(0)
    tap_gradient(0)
    wait_gpre(1)
    weight_gradient(1)
    stencil_gradient(1)
    sum_over_y(1)
    tap_gradient(1)
    for k in (4, 3, 5, 2, 6, 1, 7, 0):
        to = (y + k) % 8
        for turn in range(2):
            to_core = (core + turn) % 2
            if k or turn:
                send(
                    kg.at[to_core, to // 2, to % 2], kg_got.at[k, turn],
                    ky_send.at[k, turn], ky_recv.at[k, turn], device_at(x, zl, to_core, zh, to),
                )

    def gradient(tile):
        lanes = lanes_of(tile)
        tap = tap_of(tile)
        for r in range(4):
            pieces = []
            for i in range(2):
                for q in range(3):
                    total = None
                    start = 72 * i + 24 * q
                    for u in (-1, 0, 1):
                        if 0 <= r - u < 4:
                            term = (
                                tap(0, u, 0) * ga[r - u, start : start + 24, lanes]
                                + tap(0, u, 1) * ga_moved[r - u, i, 24 * q + 8 : 24 * q + 32, lanes]
                                + tap(0, u, -1) * ga_moved[r - u, i, 24 * q + 32 : 24 * q + 56, lanes]
                            )
                            total = term if total is None else total + term
                        if 0 <= r - 2 * u < 4:
                            for v in (-1, 0, 1):
                                if 0 <= q - v < 3:
                                    begin = start - 24 * v
                                    term = tap(1, u, v) * gb[r - 2 * u, begin : begin + 24, lanes]
                                    total = term if total is None else total + term
                    pieces.append(total)
            fg_send[r, :, lanes] = jnp.concatenate(pieces, axis=0).astype(BF16)

    for side in range(2):
        pl.loop(2 * side, 2 * side + 2)(gradient)
        for k in (2, 1, 3):
            send(
                fg_send.at[(x + k) % 4, :, sides[side]], fgrad.at[:, channels(x, side)],
                o_send.at[side, k], o_recv.at[side, k], x_peer(k),
            )
    own_grad = [
        pltpu.make_async_copy(
            fg_send.at[x, :, sides[side]], fgrad.at[:, channels(x, side)], own_sem.at[side]
        )
        for side in range(2)
    ]
    for copy in own_grad:
        copy.start()

    home_z = y // 4
    home_y = 2 * x + (y // 2) % 2

    def sum_over_z(b):
        for k in range(1, 8):
            remote(
                wg_y.at[b, k], wg_y_got.at[b, k], y_send.at[b, k], y_recv.at[b, k], mate
            ).wait_recv()
        total = wg_y[b, 0].astype(F32)
        for k in range(1, 8):
            total = total + wg_y_got[b, k].astype(F32)
        for h in range(2):
            wg_z[2 * b + h] = total[16 * h : 16 * h + 16].astype(BF16)
            send_if(
                jnp.logical_or(zl != 1 + 2 * b + h, zh != home_z),
                wg_z.at[2 * b + h], wg_z_got.at[z], z_send.at[2 * b + h], z_recv,
                device_at(x, 1 + 2 * b + h, core, home_z, y),
            )

    sum_over_z(0)
    sum_over_z(1)
    total = kg[core, y // 2, y % 2]
    for k in range(8):
        for turn in range(2):
            if k or turn:
                remote(
                    kg.at[0, 0, 0], kg_got.at[k, turn], ky_send.at[k, turn], ky_recv.at[k, turn], mate
                ).wait_recv()
                total = total + kg_got[k, turn]
    kg_z[...] = total
    send_if(
        jnp.logical_or(zl != 5, zh != home_z),
        kg_z, kg_z_got.at[z], kz_send, kz_recv, device_at(x, 5, core, home_z, y),
    )

    half = y % 2
    sums_weights = (zl > 0) & (zl < 5)
    sums_taps = zl == 5

    def spread(src, dst, send_sems, recv_sem, targets, start):
        for n, (same, target) in enumerate(targets):
            copy = remote(src, dst, send_sems.at[n], recv_sem, target)

            @pl.when(jnp.logical_not(same))
            def _(copy=copy):
                copy.start() if start else copy.wait_send()

            if start:
                here = pltpu.make_async_copy(src, dst, recv_sem)

                @pl.when(same)
                def _(here=here):
                    here.start()

    def planes():
        return [
            ((x == n) & (home_y == y), device_at(n, zl, core, home_z, home_y)) for n in range(4)
        ]

    def along_z():
        return [(zl == n, device_at(x, n, core, zh, y)) for n in range(6)]

    def first(weights, start):
        if weights:
            spread(wg_red, mid.at[half], b_send, b_recv, planes(), start)
        else:
            spread(kg_red, kmid.at[half], kb_send, kb_recv, planes(), start)

    def second(weights, start):
        if weights:
            spread(mid, fin.at[core, zl - 1], d_send, d_recv, along_z(), start)
        else:
            spread(kmid, kfin.at[core], kd_send, kd_recv, along_z(), start)

    @pl.when(sums_weights & (zh == home_z))
    def _():
        local_wait(wg_z_got, z_recv)
        total = wg_z_got[0].astype(F32)
        for n in range(1, 12):
            total = total + wg_z_got[n].astype(F32)
        wg_red[...] = (total * FACTOR).astype(BF16)
        first(True, True)

    @pl.when(sums_taps & (zh == home_z))
    def _():
        local_wait(kg_z_got, kz_recv)
        total = kg_z_got[0]
        for n in range(1, 12):
            total = total + kg_z_got[n]
        kg_red[...] = total * FACTOR
        first(False, True)

    @pl.when(sums_weights)
    def _():
        local_wait(mid, b_recv)
        second(True, True)

    @pl.when(sums_taps)
    def _():
        local_wait(kmid, kb_recv)
        second(False, True)

    local_wait(fin.at[core], d_recv)
    send(fin.at[core], fin.at[core], e_send, e_recv, mate)
    local_wait(kfin.at[core], kd_recv)
    send(kfin.at[core], kfin.at[core], ke_send, ke_recv, mate)
    remote(fin.at[core], fin.at[1 - core], e_send, e_recv, mate).wait_recv()
    remote(kfin.at[core], kfin.at[1 - core], ke_send, ke_recv, mate).wait_recv()
    for c in range(2):
        for h in range(2):
            for j in range(4):
                start = 64 * c + 32 * h + 16 * (j % 2)
                pgrad[j // 2, start : start + 16] = fin[c, j, h].astype(F32)
    for b in range(2):
        for t in range(9):
            kgrad[t, b : b + 1] = kfin[t // 8, b, t % 8 : t % 8 + 1]

    @pl.when(sums_weights & (zh == home_z))
    def _():
        first(True, False)

    @pl.when(sums_taps & (zh == home_z))
    def _():
        first(False, False)

    @pl.when(sums_weights)
    def _():
        second(True, False)

    @pl.when(sums_taps)
    def _():
        second(False, False)

    for copy in own_grad:
        copy.wait()
    for k in (1, 3, 2):
        for side in range(2):
            remote(
                fg_send.at[k, :, sides[side]], fgrad.at[:, channels((x - k + 4) % 4, side)],
                o_send.at[side, k], o_recv.at[side, k], x_peer(k),
            ).wait_recv()
    finish()


def hand_over(*refs):
    arrays, results, sems = refs[:4], refs[4:8], refs[8]
    copies = [
        pltpu.make_async_copy(array, result, sems.at[n])
        for n, (array, result) in enumerate(zip(arrays, results))
    ]
    for copy in copies:
        copy.start()
    for copy in copies:
        copy.wait()


def body(features, pointwise, depthwise, cotangent):
    shape = features.shape
    anywhere = pl.BlockSpec(memory_space=pl.ANY)
    vmem = pl.BlockSpec(memory_space=pltpu.VMEM)
    dma = pltpu.SemaphoreType.DMA
    out, fgrad, pgrad, kgrad = pl.pallas_call(
        kernel,
        out_shape=(
            pltpu.VMEM((CELLS, 2 * CO), BF16),
            pltpu.VMEM((CELLS, C), BF16),
            pltpu.VMEM((2, LANES, CO), F32),
            pltpu.VMEM((9, 2, LANES), F32),
        ),
        in_specs=[anywhere] * 4,
        out_specs=(vmem, vmem, vmem, vmem),
        scratch_shapes=[
            pltpu.VMEM((4, CELLS, PART), BF16),
            pltpu.VMEM((CELLS, 2 * CO), BF16),
            pltpu.VMEM((4, CELLS, PART), F32),
            pltpu.VMEM((4, 2, 112, PART), F32),
            pltpu.VMEM((4, 9, 2, LANES), BF16),
            pltpu.VMEM((2, 4, CELLS, PART), BF16),
            pltpu.VMEM((2, 4, 2, 64, CO), BF16),
            pltpu.VMEM((2, 16, CO), BF16),
            pltpu.VMEM((9, 2, LANES), BF16),
            pltpu.VMEM((2, CELLS, CO), F32),
            pltpu.VMEM((2, 4, CELLS, CO), BF16),
            pltpu.VMEM((2, 4, CELLS, CO), BF16),
            pltpu.VMEM((2, 4, CELLS, CO), BF16),
            pltpu.VMEM((4, CELLS, PART), F32),
            pltpu.VMEM((4, 2, 112, PART), F32),
            pltpu.VMEM((4, CELLS, PART), F32),
            pltpu.VMEM((4, CELLS, PART), BF16),
            pltpu.VMEM((2, 2, 4, 64, CO), F32),
            pltpu.VMEM((2, 2, 4, 64, CO), BF16),
            pltpu.VMEM((2, 4, 64, CO), BF16),
            pltpu.VMEM((2, 8, 32, CO), BF16),
            pltpu.VMEM((2, 8, 32, CO), BF16),
            pltpu.VMEM((4, 16, CO), BF16),
            pltpu.VMEM((12, 16, CO), BF16),
            pltpu.VMEM((16, CO), BF16),
            pltpu.VMEM((2, 4, 2, 8, LANES), F32),
            pltpu.VMEM((8, 2, 8, LANES), F32),
            pltpu.VMEM((8, LANES), F32),
            pltpu.VMEM((12, 8, LANES), F32),
            pltpu.VMEM((8, LANES), F32),
            pltpu.VMEM((2, 16, CO), BF16),
            pltpu.VMEM((2, 8, LANES), F32),
            pltpu.VMEM((2, 4, 2, 16, CO), BF16),
            pltpu.VMEM((2, 2, 8, LANES), F32),
            dma((2, 4)), dma((2, 4)), dma((2,)), dma(()),
            dma((3,)), dma((3,)),
            dma((32,)), dma((2,)),
            dma((16,)), dma((4,)),
            dma((2,)), dma((2,)),
            dma((2, 4)), dma((2, 4)),
            dma((2, 4)), dma((2, 4)),
            dma((2, 4)), dma((2, 4)),
            dma((2,)), dma((2,)),
            dma((2, 8)), dma((2, 8)),
            dma((4,)), dma(()),
            dma((4,)), dma(()),
            dma((6,)), dma(()),
            dma(()), dma(()),
            dma((8, 2)), dma((8, 2)),
            dma(()), dma(()),
            dma((4,)), dma(()),
            dma((6,)), dma(()),
            dma(()), dma(()),
        ],
        compiler_params=pltpu.CompilerParams(
            collective_id=0, has_side_effects=True, vmem_limit_bytes=60 * 1024 * 1024
        ),
    )(
        features.reshape(CELLS, C), pointwise, depthwise.transpose(1, 0, 2), cotangent.reshape(CELLS, 2 * CO)
    )
    made = (out, fgrad, pgrad, kgrad)
    out, fgrad, pgrad, kgrad = pl.pallas_call(
        hand_over,
        out_shape=tuple(jax.ShapeDtypeStruct(m.shape, m.dtype) for m in made),
        in_specs=[anywhere] * 4,
        out_specs=(anywhere,) * 4,
        scratch_shapes=[dma((4,))],
        compiler_params=pltpu.CompilerParams(vmem_limit_bytes=1024 * 1024),
    )(*made)
    return (
        out.reshape(*shape[:3], 2 * CO), fgrad.reshape(shape), pgrad, kgrad.transpose(1, 0, 2)
    )


def solution(mesh):
    return jax.shard_map(
        body,
        mesh=mesh,
        in_specs=(
            P("dp", "space", None, None),
            P(None, "dp", None),
            P(None, None, "dp"),
            P("dp", "space", None, None),
        ),
        out_specs=(
            P("dp", "space", None, None),
            P("dp", "space", None, None),
            P(None, "dp", None),
            P(None, None, "dp"),
        ),
        check_vma=False,
    )
```

```python
import jax
import jax.numpy as jnp
from jax import lax
from jax.experimental import pallas as pl
from jax.experimental.pallas import tpu as pltpu
from jax.sharding import PartitionSpec as P

C = 2048
CO = 256
CELLS = 144
LANES = 128
PART = 512
BF16 = jnp.bfloat16
F32 = jnp.float32
MESH = pl.DeviceIdType.MESH
FACTOR = 1.0 / (110592.0**0.5)


def device_at(x, z_low, core, z_high, y):
    return {"space": (x * 6 + z_low) * 2 + core, "dp": z_high * 8 + y}


def local_wait(ref, sem):
    pltpu.make_async_copy(ref, ref, sem).wait()


def kernel(
    feat, pw, kin, cot,
    out, fgrad, pgrad, kgrad,
    rows, cot_here, wide, moved, taps, dcv, wts, away_w, away_k,
    own_pre, send_pre, got_pre, gpre, ga, ga_moved, gb, fg_send,
    wg_wide, wg, wg_core, wg_y, wg_y_got, wg_z, wg_z_got, wg_red,
    kg, kg_got, kg_z, kg_z_got, kg_red, mid, kmid, fin, kfin,
    f_send, f_recv, own_sem, cot_sem, a_send, a_recv, w_send, w_recv, k_send, k_recv, wc_send, wc_recv,
    p_send, p_recv, g_send, g_recv, o_send, o_recv,
    c_send, c_recv, y_send, y_recv, z_send, z_recv, b_send, b_recv, d_send, d_recv, e_send, e_recv,
    ky_send, ky_recv, kz_send, kz_recv, kb_send, kb_recv, kd_send, kd_recv, ke_send, ke_recv,
):
    space = lax.axis_index("space")
    dp = lax.axis_index("dp")
    x = space // 12
    zl = (space // 2) % 6
    core = space % 2
    zh = dp // 8
    y = dp % 8
    z = zh * 6 + zl
    plane = y // 2
    at_home = x == plane
    mate = device_at(x, zl, 1 - core, zh, y)
    sent = []

    def remote(src, dst, send_sem, recv_sem, target):
        return pltpu.make_async_remote_copy(
            src_ref=src, dst_ref=dst, send_sem=send_sem, recv_sem=recv_sem,
            device_id=target, device_id_type=MESH,
        )

    def send(src, dst, send_sem, recv_sem, target):
        copy = remote(src, dst, send_sem, recv_sem, target)
        copy.start()
        sent.append((None, copy))

    def send_if(cond, src, dst, send_sem, recv_sem, target):
        copy = remote(src, dst, send_sem, recv_sem, target)
        here = pltpu.make_async_copy(src, dst, recv_sem)

        @pl.when(cond)
        def _():
            copy.start()

        @pl.when(jnp.logical_not(cond))
        def _():
            here.start()

        sent.append((cond, copy))

    def finish():
        for cond, copy in sent:
            if cond is None:
                copy.wait_send()
            else:

                @pl.when(cond)
                def _(copy=copy):
                    copy.wait_send()

    def x_peer(k):
        return device_at((x + k) % 4, zl, core, zh, y)

    def z_peer(k):
        other = (z + k) % 12
        return device_at(x, other % 6, core, other // 6, y)

    sides = (slice(0, 256), slice(256, 512))

    def channels(of_x, side):
        return pl.ds(pl.multiple_of(side * 1024 + of_x * 256, 256), 256)

    barrier = pltpu.get_barrier_semaphore()

    def greet(target):
        pl.semaphore_signal(barrier, inc=1, device_id=target, device_id_type=MESH)

    count = 0
    for k in (1, 3, 2):
        greet(x_peer(k))
        count += 1
    greet(mate)
    count += 1
    for k in range(1, 12):
        greet(z_peer(k))
        count += 1
    for k in range(1, 8):
        greet(device_at(plane, zl, core, zh, (y + k) % 8))
        count += 1
    for other in range(4):
        for near in range(2):
            target_y = 2 * x + near
            same = jnp.logical_and(other == x, target_y == y)

            @pl.when(jnp.logical_not(same))
            def _(other=other, target_y=target_y):
                greet(device_at(other, zl, core, zh, target_y))

    @pl.when(jnp.logical_not(at_home))
    def _():
        greet(device_at(plane, zl, core, zh, y))

    count += 9
    pl.semaphore_wait(barrier, count - 2 * at_home.astype(jnp.int32))

    def send_rows(side):
        for k in (2, 1, 3):
            send(
                feat.at[:, channels((x + k) % 4, side)], rows.at[x, :, sides[side]],
                f_send.at[side, k], f_recv.at[side, k], x_peer(k),
            )

    piece = pl.ds(pl.multiple_of(core * 64 + x * 16, 16), 16)
    partner = device_at(x, (zl + 3) % 6, core, 1 - zh, y)
    send(kin, away_k, a_send.at[2], a_recv.at[2], partner)
    for b in range(2):
        send(pw.at[b, piece], away_w.at[b], a_send.at[b], a_recv.at[b], partner)
    near_slot = zh * 2 + y % 2
    far_slot = (1 - zh) * 2 + y % 2
    not_home = jnp.logical_not(at_home)

    def spread_taps(src, slot, base):
        for k in range(8):
            target = device_at(plane, zl, core, zh, (y + k) % 8)
            if k == 0:
                here = pltpu.make_async_copy(src, taps.at[slot], k_recv.at[slot])

                @pl.when(at_home)
                def _(here=here):
                    here.start()
            else:
                copy = remote(src, taps.at[slot], k_send.at[base + k], k_recv.at[slot], target)

                @pl.when(at_home)
                def _(copy=copy):
                    copy.start()

                sent.append((at_home, copy))

    def spread_weights(b, src, slot, base):
        for k in range(8):
            target = device_at(plane, zl, core, zh, (y + k) % 8)
            dst = wts.at[b, slot, core, pl.ds(pl.multiple_of(x * 16, 16), 16)]
            if k == 0:
                send_if(not_home, src, dst, w_send.at[base], w_recv.at[b], target)
            else:
                send(src, dst, w_send.at[base + k], w_recv.at[b], target)

    spread_taps(kin, near_slot, 0)
    for b in range(2):
        spread_weights(b, pw.at[b, piece], near_slot, 16 * b)
    send_rows(0)
    own_rows = [
        pltpu.make_async_copy(
            feat.at[:, channels(x, side)], rows.at[x, :, sides[side]], own_sem.at[side]
        )
        for side in range(2)
    ]
    for copy in own_rows:
        copy.start()
    cot_copy = pltpu.make_async_copy(cot, cot_here, cot_sem)
    cot_copy.start()
    border = jnp.zeros((24, PART), F32)
    for r in range(4):
        for i in range(2):
            for array in (moved, ga_moved):
                array[r, i, 0:24] = border
                array[r, i, 88:112] = border
    kg[...] = jnp.zeros_like(kg)
    remote(kin, away_k, a_send.at[2], a_recv.at[2], partner).wait_recv()
    spread_taps(away_k, far_slot, 8)
    for b in range(2):
        remote(pw.at[b, piece], away_w.at[b], a_send.at[b], a_recv.at[b], partner).wait_recv()
        spread_weights(b, away_w.at[b], far_slot, 16 * b + 8)
    send_rows(1)

    def tap_of(tile):
        weights = taps[tile].astype(F32)

        def tap(b, u, v):
            t = (u + 1) * 3 + v + 1
            return weights[t, b : b + 1]

        return tap

    def lanes_of(tile):
        return pl.ds(pl.multiple_of(tile * LANES, LANES), LANES)

    def stencils_a(tile):
        lanes = lanes_of(tile)
        for r in range(4):
            value = rows[r, :, lanes].astype(F32)
            wide[r, :, lanes] = value
            for i in range(2):
                moved[r, i, 20:92, lanes] = value[72 * i : 72 * i + 72]
        tap = tap_of(tile)
        for r in range(4):
            pieces = []
            for i in range(2):
                for q in range(3):
                    total = None
                    for u in (-1, 0, 1):
                        if not 0 <= r + u < 4:
                            continue
                        term = (
                            tap(0, u, 0) * wide[r + u, 72 * i + 24 * q : 72 * i + 24 * q + 24, lanes]
                            + tap(0, u, -1) * moved[r + u, i, 24 * q + 8 : 24 * q + 32, lanes]
                            + tap(0, u, 1) * moved[r + u, i, 24 * q + 32 : 24 * q + 56, lanes]
                        )
                        total = term if total is None else total + term
                    pieces.append(total)
            dcv[0, r, :, lanes] = jnp.concatenate(pieces, axis=0).astype(BF16)

    def stencils_b(tile):
        lanes = lanes_of(tile)
        tap = tap_of(tile)
        for r in range(4):
            pieces = []
            for i in range(2):
                for q in range(3):
                    total = None
                    for u in (-1, 0, 1):
                        if not 0 <= r + 2 * u < 4:
                            continue
                        for v in (-1, 0, 1):
                            if not 0 <= q + v < 3:
                                continue
                            start = 72 * i + 24 * (q + v)
                            term = tap(1, u, v) * wide[r + 2 * u, start : start + 24, lanes]
                            total = term if total is None else total + term
                    pieces.append(total)
            dcv[1, r, :, lanes] = jnp.concatenate(pieces, axis=0).astype(BF16)

    for slot in range(4):
        local_wait(taps.at[slot], k_recv.at[slot])
    for side in range(2):
        own_rows[side].wait()
        for k in (1, 3, 2):
            remote(
                rows.at[x, :, sides[side]], rows.at[(x - k + 4) % 4, :, sides[side]],
                f_send.at[side, k], f_recv.at[side, k], x_peer(k),
            ).wait_recv()
        pl.loop(2 * side, 2 * side + 2)(stencils_a)

    def trade_weights(b):
        local_wait(wts.at[b, :, core], w_recv.at[b])
        send(wts.at[b, :, core], wts.at[b, :, core], wc_send.at[b], wc_recv.at[b], mate)

    def wait_weights(b):
        remote(
            wts.at[b, :, core], wts.at[b, :, 1 - core], wc_send.at[b], wc_recv.at[b], mate
        ).wait_recv()

    trade_weights(0)
    pl.loop(0, 4)(stencils_b)
    trade_weights(1)

    def products(b):
        for k in (2, 1, 3, 0):
            part = jnp.dot(
                dcv[b, (x + k) % 4], wts[b].reshape(PART, CO), preferred_element_type=F32
            )
            if k:
                send_pre[b, k] = part.astype(BF16)
                send(send_pre.at[b, k], got_pre.at[b, k], p_send.at[b, k], p_recv.at[b, k], x_peer(k))
            else:
                own_pre[b] = part

    wait_weights(0)
    products(0)
    wait_weights(1)
    products(1)
    cot_copy.wait()
    for b in range(2):
        cols = slice(b * CO, (b + 1) * CO)
        for k in (1, 3, 2):
            remote(
                send_pre.at[b, k], got_pre.at[b, k], p_send.at[b, k], p_recv.at[b, k], x_peer(k)
            ).wait_recv()
        pre = own_pre[b]
        for k in (1, 3, 2):
            pre = pre + got_pre[b, k].astype(F32)
        sig = 1.0 / (1.0 + jnp.exp(-pre))
        gpre[b, x] = (cot_here[:, cols].astype(F32) * sig * (1.0 + pre * (1.0 - sig))).astype(BF16)
        for k in (2, 1, 3):
            send(gpre.at[b, x], gpre.at[b, x], g_send.at[b, k], g_recv.at[b, k], x_peer(k))
        out[:, cols] = (pre * sig).astype(BF16)

    def wait_gpre(b):
        for k in (1, 3, 2):
            remote(
                gpre.at[b, x], gpre.at[b, (x - k + 4) % 4], g_send.at[b, k], g_recv.at[b, k], x_peer(k)
            ).wait_recv()

    def weight_gradient(b):
        @pl.loop(0, 4)
        def _(tile):
            grad = lax.dot_general(
                dcv[b, :, :, lanes_of(tile)].reshape(4 * CELLS, LANES),
                gpre[b].reshape(4 * CELLS, CO),
                (((0,), (0,)), ((), ())),
                preferred_element_type=F32,
            )
            for half in range(2):
                block = grad[64 * half : 64 * half + 64]
                wg_wide[b, half, tile] = block
                wg[b, half, tile] = block.astype(BF16)

        send(wg.at[b, 1 - core], wg_core.at[b], c_send.at[b], c_recv.at[b], mate)

    def stencil_gradient(b):
        @pl.loop(0, 4)
        def _(r):
            back = lax.dot_general(
                gpre[b, r], wts[b].reshape(PART, CO), (((1,), (1,)), ((), ())),
                preferred_element_type=F32,
            )
            if b:
                gb[r] = back
            else:
                ga[r] = back
                for i in range(2):
                    ga_moved[r, i, 20:92] = back[72 * i : 72 * i + 72]

    def sum_over_y(b):
        remote(
            wg.at[b, 1 - core], wg_core.at[b], c_send.at[b], c_recv.at[b], mate
        ).wait_recv()
        for k in (4, 3, 5, 2, 6, 1, 7, 0):
            to = (y + k) % 8
            slot = to // 2
            part = pl.ds(pl.multiple_of((to % 2) * 32, 32), 32)
            wg_y[b, k] = (
                wg_wide[b, core, slot, part] + wg_core[b, slot, part].astype(F32)
            ).astype(BF16)
            if k:
                send(
                    wg_y.at[b, k], wg_y_got.at[b, k], y_send.at[b, k], y_recv.at[b, k],
                    device_at(x, zl, core, zh, to),
                )

    def tap_gradient(b):
        step = b + 1

        @pl.loop(0, 4)
        def _(tile):
            lanes = lanes_of(tile)
            for u in (-1, 0, 1):
                sums = [None, None, None]
                for r in range(4):
                    if not 0 <= r + step * u < 4:
                        continue
                    for i in range(2):
                        for q in range(3):
                            start = 72 * i + 24 * q
                            if b:
                                grad = gb[r, start : start + 24, lanes]
                            else:
                                grad = ga[r, start : start + 24, lanes]
                            for v in (-1, 0, 1):
                                if b:
                                    if not 0 <= q + v < 3:
                                        continue
                                    source = wide[r + 2 * u, start + 24 * v : start + 24 * v + 24, lanes]
                                elif v == 0:
                                    source = wide[r + u, start : start + 24, lanes]
                                else:
                                    begin = 24 * q + 20 + 12 * v
                                    source = moved[r + u, i, begin : begin + 24, lanes]
                                term = source * grad
                                term = term[0:8] + term[8:16] + term[16:24]
                                old = sums[v + 1]
                                sums[v + 1] = term if old is None else old + term
                for v in (-1, 0, 1):
                    t = (u + 1) * 3 + v + 1
                    total = jnp.sum(sums[v + 1], axis=0, keepdims=True)
                    kg[t // 8, tile, b, t % 8 : t % 8 + 1] = total

    wait_gpre(0)
    weight_gradient(0)
    stencil_gradient(0)
    sum_over_y(0)
    wait_gpre(1)
    weight_gradient(1)
    stencil_gradient(1)
    sum_over_y(1)
    tap_gradient(0)
    tap_gradient(1)
    for k in (4, 3, 5, 2, 6, 1, 7, 0):
        to = (y + k) % 8
        for turn in range(2):
            to_core = (core + turn) % 2
            if k or turn:
                send(
                    kg.at[to_core, to // 2, to % 2], kg_got.at[k, turn],
                    ky_send.at[k, turn], ky_recv.at[k, turn], device_at(x, zl, to_core, zh, to),
                )

    def gradient(tile):
        lanes = lanes_of(tile)
        tap = tap_of(tile)
        for r in range(4):
            pieces = []
            for i in range(2):
                for q in range(3):
                    total = None
                    start = 72 * i + 24 * q
                    for u in (-1, 0, 1):
                        if 0 <= r - u < 4:
                            term = (
                                tap(0, u, 0) * ga[r - u, start : start + 24, lanes]
                                + tap(0, u, 1) * ga_moved[r - u, i, 24 * q + 8 : 24 * q + 32, lanes]
                                + tap(0, u, -1) * ga_moved[r - u, i, 24 * q + 32 : 24 * q + 56, lanes]
                            )
                            total = term if total is None else total + term
                        if 0 <= r - 2 * u < 4:
                            for v in (-1, 0, 1):
                                if 0 <= q - v < 3:
                                    begin = start - 24 * v
                                    term = tap(1, u, v) * gb[r - 2 * u, begin : begin + 24, lanes]
                                    total = term if total is None else total + term
                    pieces.append(total)
            fg_send[r, :, lanes] = jnp.concatenate(pieces, axis=0).astype(BF16)

    for side in range(2):
        pl.loop(2 * side, 2 * side + 2)(gradient)
        for k in (2, 1, 3):
            send(
                fg_send.at[(x + k) % 4, :, sides[side]], fgrad.at[:, channels(x, side)],
                o_send.at[side, k], o_recv.at[side, k], x_peer(k),
            )
    own_grad = [
        pltpu.make_async_copy(
            fg_send.at[x, :, sides[side]], fgrad.at[:, channels(x, side)], own_sem.at[side]
        )
        for side in range(2)
    ]
    for copy in own_grad:
        copy.start()

    home_z = y // 4
    home_y = 2 * x + (y // 2) % 2

    def sum_over_z(b):
        for k in range(1, 8):
            remote(
                wg_y.at[b, k], wg_y_got.at[b, k], y_send.at[b, k], y_recv.at[b, k], mate
            ).wait_recv()
        total = wg_y[b, 0].astype(F32)
        for k in range(1, 8):
            total = total + wg_y_got[b, k].astype(F32)
        for h in range(2):
            wg_z[2 * b + h] = total[16 * h : 16 * h + 16].astype(BF16)
            send_if(
                jnp.logical_or(zl != 1 + 2 * b + h, zh != home_z),
                wg_z.at[2 * b + h], wg_z_got.at[z], z_send.at[2 * b + h], z_recv,
                device_at(x, 1 + 2 * b + h, core, home_z, y),
            )

    sum_over_z(0)
    sum_over_z(1)
    total = kg[core, y // 2, y % 2]
    for k in range(8):
        for turn in range(2):
            if k or turn:
                remote(
                    kg.at[0, 0, 0], kg_got.at[k, turn], ky_send.at[k, turn], ky_recv.at[k, turn], mate
                ).wait_recv()
                total = total + kg_got[k, turn]
    kg_z[...] = total
    send_if(
        jnp.logical_or(zl != 5, zh != home_z),
        kg_z, kg_z_got.at[z], kz_send, kz_recv, device_at(x, 5, core, home_z, y),
    )

    half = y % 2
    sums_weights = (zl > 0) & (zl < 5)
    sums_taps = zl == 5

    def spread(src, dst, send_sems, recv_sem, targets, start):
        for n, (same, target) in enumerate(targets):
            copy = remote(src, dst, send_sems.at[n], recv_sem, target)

            @pl.when(jnp.logical_not(same))
            def _(copy=copy):
                copy.start() if start else copy.wait_send()

            if start:
                here = pltpu.make_async_copy(src, dst, recv_sem)

                @pl.when(same)
                def _(here=here):
                    here.start()

    def planes():
        return [
            ((x == n) & (home_y == y), device_at(n, zl, core, home_z, home_y)) for n in range(4)
        ]

    def along_z():
        return [(zl == n, device_at(x, n, core, zh, y)) for n in range(6)]

    def first(weights, start):
        if weights:
            spread(wg_red, mid.at[half], b_send, b_recv, planes(), start)
        else:
            spread(kg_red, kmid.at[half], kb_send, kb_recv, planes(), start)

    def second(weights, start):
        if weights:
            spread(mid, fin.at[core, zl - 1], d_send, d_recv, along_z(), start)
        else:
            spread(kmid, kfin.at[core], kd_send, kd_recv, along_z(), start)

    @pl.when(sums_weights & (zh == home_z))
    def _():
        local_wait(wg_z_got, z_recv)
        total = wg_z_got[0].astype(F32)
        for n in range(1, 12):
            total = total + wg_z_got[n].astype(F32)
        wg_red[...] = (total * FACTOR).astype(BF16)
        first(True, True)

    @pl.when(sums_taps & (zh == home_z))
    def _():
        local_wait(kg_z_got, kz_recv)
        total = kg_z_got[0]
        for n in range(1, 12):
            total = total + kg_z_got[n]
        kg_red[...] = total * FACTOR
        first(False, True)

    @pl.when(sums_weights)
    def _():
        local_wait(mid, b_recv)
        second(True, True)

    @pl.when(sums_taps)
    def _():
        local_wait(kmid, kb_recv)
        second(False, True)

    local_wait(fin.at[core], d_recv)
    send(fin.at[core], fin.at[core], e_send, e_recv, mate)
    local_wait(kfin.at[core], kd_recv)
    send(kfin.at[core], kfin.at[core], ke_send, ke_recv, mate)

    def place(c):
        for h in range(2):
            for j in range(4):
                start = pl.multiple_of(64 * c + 32 * h + 16 * (j % 2), 16)
                pgrad[j // 2, pl.ds(start, 16)] = fin[c, j, h].astype(F32)

    place(core)
    remote(fin.at[core], fin.at[1 - core], e_send, e_recv, mate).wait_recv()
    place(1 - core)
    remote(kfin.at[core], kfin.at[1 - core], ke_send, ke_recv, mate).wait_recv()
    for b in range(2):
        for t in range(9):
            kgrad[t, b : b + 1] = kfin[t // 8, b, t % 8 : t % 8 + 1]

    @pl.when(sums_weights & (zh == home_z))
    def _():
        first(True, False)

    @pl.when(sums_taps & (zh == home_z))
    def _():
        first(False, False)

    @pl.when(sums_weights)
    def _():
        second(True, False)

    @pl.when(sums_taps)
    def _():
        second(False, False)

    for copy in own_grad:
        copy.wait()
    for k in (1, 3, 2):
        for side in range(2):
            remote(
                fg_send.at[k, :, sides[side]], fgrad.at[:, channels((x - k + 4) % 4, side)],
                o_send.at[side, k], o_recv.at[side, k], x_peer(k),
            ).wait_recv()
    finish()


def hand_over(*refs):
    arrays, results, sems = refs[:4], refs[4:8], refs[8]
    copies = [
        pltpu.make_async_copy(array, result, sems.at[n])
        for n, (array, result) in enumerate(zip(arrays, results))
    ]
    for copy in copies:
        copy.start()
    for copy in copies:
        copy.wait()


def body(features, pointwise, depthwise, cotangent):
    shape = features.shape
    anywhere = pl.BlockSpec(memory_space=pl.ANY)
    vmem = pl.BlockSpec(memory_space=pltpu.VMEM)
    dma = pltpu.SemaphoreType.DMA
    out, fgrad, pgrad, kgrad = pl.pallas_call(
        kernel,
        out_shape=(
            pltpu.VMEM((CELLS, 2 * CO), BF16),
            pltpu.VMEM((CELLS, C), BF16),
            pltpu.VMEM((2, LANES, CO), F32),
            pltpu.VMEM((9, 2, LANES), F32),
        ),
        in_specs=[anywhere] * 4,
        out_specs=(vmem, vmem, vmem, vmem),
        scratch_shapes=[
            pltpu.VMEM((4, CELLS, PART), BF16),
            pltpu.VMEM((CELLS, 2 * CO), BF16),
            pltpu.VMEM((4, CELLS, PART), F32),
            pltpu.VMEM((4, 2, 112, PART), F32),
            pltpu.VMEM((4, 9, 2, LANES), BF16),
            pltpu.VMEM((2, 4, CELLS, PART), BF16),
            pltpu.VMEM((2, 4, 2, 64, CO), BF16),
            pltpu.VMEM((2, 16, CO), BF16),
            pltpu.VMEM((9, 2, LANES), BF16),
            pltpu.VMEM((2, CELLS, CO), F32),
            pltpu.VMEM((2, 4, CELLS, CO), BF16),
            pltpu.VMEM((2, 4, CELLS, CO), BF16),
            pltpu.VMEM((2, 4, CELLS, CO), BF16),
            pltpu.VMEM((4, CELLS, PART), F32),
            pltpu.VMEM((4, 2, 112, PART), F32),
            pltpu.VMEM((4, CELLS, PART), F32),
            pltpu.VMEM((4, CELLS, PART), BF16),
            pltpu.VMEM((2, 2, 4, 64, CO), F32),
            pltpu.VMEM((2, 2, 4, 64, CO), BF16),
            pltpu.VMEM((2, 4, 64, CO), BF16),
            pltpu.VMEM((2, 8, 32, CO), BF16),
            pltpu.VMEM((2, 8, 32, CO), BF16),
            pltpu.VMEM((4, 16, CO), BF16),
            pltpu.VMEM((12, 16, CO), BF16),
            pltpu.VMEM((16, CO), BF16),
            pltpu.VMEM((2, 4, 2, 8, LANES), F32),
            pltpu.VMEM((8, 2, 8, LANES), F32),
            pltpu.VMEM((8, LANES), F32),
            pltpu.VMEM((12, 8, LANES), F32),
            pltpu.VMEM((8, LANES), F32),
            pltpu.VMEM((2, 16, CO), BF16),
            pltpu.VMEM((2, 8, LANES), F32),
            pltpu.VMEM((2, 4, 2, 16, CO), BF16),
            pltpu.VMEM((2, 2, 8, LANES), F32),
            dma((2, 4)), dma((2, 4)), dma((2,)), dma(()),
            dma((3,)), dma((3,)),
            dma((32,)), dma((2,)),
            dma((16,)), dma((4,)),
            dma((2,)), dma((2,)),
            dma((2, 4)), dma((2, 4)),
            dma((2, 4)), dma((2, 4)),
            dma((2, 4)), dma((2, 4)),
            dma((2,)), dma((2,)),
            dma((2, 8)), dma((2, 8)),
            dma((4,)), dma(()),
            dma((4,)), dma(()),
            dma((6,)), dma(()),
            dma(()), dma(()),
            dma((8, 2)), dma((8, 2)),
            dma(()), dma(()),
            dma((4,)), dma(()),
            dma((6,)), dma(()),
            dma(()), dma(()),
        ],
        compiler_params=pltpu.CompilerParams(
            collective_id=0, has_side_effects=True, vmem_limit_bytes=60 * 1024 * 1024
        ),
    )(
        features.reshape(CELLS, C), pointwise, depthwise.transpose(1, 0, 2), cotangent.reshape(CELLS, 2 * CO)
    )
    made = (out, fgrad, pgrad, kgrad)
    out, fgrad, pgrad, kgrad = pl.pallas_call(
        hand_over,
        out_shape=tuple(jax.ShapeDtypeStruct(m.shape, m.dtype) for m in made),
        in_specs=[anywhere] * 4,
        out_specs=(anywhere,) * 4,
        scratch_shapes=[dma((4,))],
        compiler_params=pltpu.CompilerParams(vmem_limit_bytes=1024 * 1024),
    )(*made)
    return (
        out.reshape(*shape[:3], 2 * CO), fgrad.reshape(shape), pgrad, kgrad.transpose(1, 0, 2)
    )


def solution(mesh):
    return jax.shard_map(
        body,
        mesh=mesh,
        in_specs=(
            P("dp", "space", None, None),
            P(None, "dp", None),
            P(None, None, "dp"),
            P("dp", "space", None, None),
        ),
        out_specs=(
            P("dp", "space", None, None),
            P("dp", "space", None, None),
            P(None, "dp", None),
            P(None, None, "dp"),
        ),
        check_vma=False,
    )
```
